256 devices in a mesh: dom: 32 (over y, x, z_hi), band: 8 (over z_lo, core).
Axes of the slice: x: 4, y: 4, z: 8 (z_hi: 2, z_lo: 4; z = z_hi * 4 + z_lo), core: 2. Of those that a mesh axis runs over, the one named last changes fastest.
Arguments:
- wavefunctions: bfloat16 [65536, 1024], P('dom', 'band'), may hold values from -4 to 4
- mass_scale: float32 [65536], P('dom'), may hold values from 0.7 to 1.4
- cell_matrices: bfloat16 [256, 512, 512], P('dom')
- connectivity: int32 [256, 512], P('dom'), may hold values from 0 to 2303, as said below
- face_index: int32 [8192], P('dom'), may hold values from 0 to 2047, as said below
Outputs:
- rotated: float32 [65536, 1024], P('dom', 'band')
The draws below stay inside these ranges and needn't reach their ends.
Inputs may be any that keep to these rules, and one draw needn't show every extreme that they name: `connectivity`: local numbers of each cell's 512 nodes within its domain: below 2048 the domain's own nodes, from 2048 on the entries of the next domain's face list in order; every local number appears in its domain, and a number may repeat. `face_index`: local numbers of 256 own nodes of each domain, in the order that the previous domain uses; a number may repeat.
All inputs are finite; a program needn't handle non-finite values.
Results may differ from the reference program's by a relative error of at most 0.011.
Values may be sent and summed in bfloat16 or wider, within the bound.
No kernel may reach another device: no remote copies, remote signals or barrier semaphores. Data moves between devices by JAX's collectives and lax.ppermute only.
A program may use at most 64 MiB of HBM per device.

```python
import math
import jax
import jax.numpy as jnp
from jax import lax

NODE_DEV = 2048
STATES = 1024
CELL_NODES = 512
DEGREE = 3
NS_ITERS = 2
CELLS_DEV = 8
FACE = 256
NODES = 65536
CELLS = 256
FACES = 8192
N_DOM = 32


def draw_wavefunctions(key, part):
    key_one = jax.random.fold_in(jax.random.fold_in(key, 5), 0)
    values = jax.random.truncated_normal(key_one, -4.0, 4.0, (NODES, STATES), jnp.float32)
    return jnp.clip(values, -4.0, 4.0).astype(jnp.bfloat16)


def draw_cell_matrices(key, part):
    key_one, key_two = jax.random.split(jax.random.fold_in(key, 3))
    cell_shape = (CELLS, CELL_NODES, CELL_NODES)
    random_part = jax.random.normal(key_one, cell_shape, jnp.float32)
    diagonal = jax.random.uniform(key_two, (CELLS, CELL_NODES), jnp.float32, 0.5, 2.5)
    symmetric = (random_part + jnp.swapaxes(random_part, 1, 2)) / (2.0 * math.sqrt(CELL_NODES))
    identity = jnp.eye(CELL_NODES, dtype=jnp.float32)
    return (symmetric + diagonal[:, :, None] * identity[None]).astype(jnp.bfloat16)


def draw_connectivity(key, part):
    domains = CELLS // CELLS_DEV
    extent = NODE_DEV + FACE

    def one_domain(domain_key):
        key_one, key_two = jax.random.split(domain_key)
        ordering = jnp.concatenate([jax.random.permutation(key_one, extent), jax.random.permutation(key_two, extent)])
        return ordering[:CELLS_DEV * CELL_NODES].reshape(CELLS_DEV, CELL_NODES)
    domain_keys = jax.random.split(jax.random.fold_in(key, 11), domains)
    return jax.vmap(one_domain)(domain_keys).reshape(CELLS, CELL_NODES).astype(jnp.int32)


def draw_face_index(key, part):
    domains = FACES // FACE

    def one_domain(domain_key):
        chosen = jax.random.permutation(domain_key, NODE_DEV)[:FACE]
        return chosen.at[0].set(NODE_DEV - 1)
    domain_keys = jax.random.split(jax.random.fold_in(key, 17), domains)
    return jax.vmap(one_domain)(domain_keys).reshape(FACES).astype(jnp.int32)


def steps_of(rng, shape, shards, least, high):
    level = 1.0
    for dim, shards_of in shards:
        draws = jax.random.uniform(jax.random.fold_in(jax.random.fold_in(rng, 6), dim), (shards_of,), jnp.float32, least / len(shards), high / len(shards))
        level = level * jnp.repeat(jnp.exp(draws), shape[dim] // shards_of).reshape((-1,) + (1,) * (len(shape) - 1 - dim))
    return level


def setup_inputs(seed: int = 0) -> dict:
    splits = jax.random.split(jax.random.key(seed), 6)
    return {
        "wavefunctions": draw_wavefunctions(jax.random.fold_in(splits[5], 71), 0),
        "mass_scale": jnp.clip(jnp.exp(math.log(1.4) - 0.6931472 * jax.random.uniform(splits[1], (NODES,), jnp.float32) ** steps_of(splits[1], (NODES,), ((0, 32),), -0.2, 0.2)), 0.7, 1.4),
        "cell_matrices": draw_cell_matrices(jax.random.fold_in(splits[5], 71), 0),
        "connectivity": draw_connectivity(jax.random.fold_in(splits[5], 71), 0),
        "face_index": draw_face_index(jax.random.fold_in(splits[5], 71), 0),
    }


def apply_hamiltonian(vectors, mass_scale, cell_matrices, connectivity, face_index):
    band_width = vectors.shape[1]
    scaled = (mass_scale[:, None] * vectors).astype(jnp.bfloat16)
    by_domain = scaled.reshape(N_DOM, NODE_DEV, band_width)
    face_lists = face_index.reshape(N_DOM, FACE)
    face_rows = jax.vmap(lambda rows_all, picks: jnp.take(rows_all, picks, axis=0))(by_domain, face_lists)
    received = jnp.concatenate([face_rows[1:], jnp.zeros_like(face_rows[:1])], axis=0)
    extended = jnp.concatenate([by_domain, received], axis=1)
    cell_blocks = cell_matrices.reshape(N_DOM, CELLS_DEV, CELL_NODES, CELL_NODES)
    link_blocks = connectivity.reshape(N_DOM, CELLS_DEV, CELL_NODES)

    def one_domain(inputs):
        extended_rows, matrices, links = inputs
        gathered = jnp.take(extended_rows, links, axis=0).astype(jnp.float32)
        products = jnp.einsum('cij,cjs->cis', matrices.astype(jnp.float32), gathered)
        assembled = jnp.zeros((NODE_DEV + FACE, band_width), jnp.float32)
        return assembled.at[links.reshape(-1)].add(products.reshape(-1, band_width))
    assembled = lax.map(one_domain, (extended, cell_blocks, link_blocks))
    own_rows = assembled[:, :NODE_DEV]
    returned = jnp.concatenate([jnp.zeros_like(assembled[:1, NODE_DEV:]), assembled[:-1, NODE_DEV:]], axis=0)
    summed = jax.vmap(lambda target, picks, extra: target.at[picks].add(extra))(own_rows, face_lists, returned)
    return mass_scale[:, None] * summed.reshape(N_DOM * NODE_DEV, band_width)

def reference(wavefunctions, mass_scale, cell_matrices, connectivity, face_index):

    def hamiltonian(vectors):
        return apply_hamiltonian(vectors, mass_scale, cell_matrices, connectivity, face_index)
    previous = wavefunctions.astype(jnp.float32)
    current = (hamiltonian(previous) - 5.0 * previous) / 5.0
    for sweep_index in range(DEGREE - 1):
        following = 2.0 * (hamiltonian(current) - 5.0 * current) / 5.0 - previous
        previous, current = (current, following)
    filtered = current
    rounded = filtered.astype(jnp.bfloat16)
    margin = jnp.dot(rounded.T, rounded, preferred_element_type=jnp.float32) / (NODE_DEV * N_DOM)
    mean_eigen = jnp.trace(margin) / STATES
    identity = jnp.eye(STATES, dtype=jnp.float32)
    current_y = margin / mean_eigen
    current_z = identity
    highest = lax.Precision.HIGHEST
    for ns_index in range(NS_ITERS):
        product = jnp.dot(current_z, current_y, precision=highest, preferred_element_type=jnp.float32)
        correction = 1.5 * identity - 0.5 * product
        current_y = jnp.dot(current_y, correction, precision=highest, preferred_element_type=jnp.float32)
        current_z = jnp.dot(current_z, correction, precision=highest, preferred_element_type=jnp.float32)
    inverse_root = current_z / jnp.sqrt(mean_eigen)
    return jnp.dot(filtered, inverse_root, precision=highest, preferred_element_type=jnp.float32)
```

```python
import functools

import jax
import jax.numpy as jnp
from jax import lax
from jax.experimental import pallas as pl
from jax.experimental.pallas import tpu as pltpu
from jax.sharding import Mesh
from jax.sharding import PartitionSpec as P

STATES = 1024
DEGREE = 3
CENTER = 5.0
HALF = 5.0
DOM = ("dom_0", "dom_1", "dom_2")
BAND = ("band_0", "band_1")
PLANE = ("dom_0", "dom_1")
COLUMN = ("dom_2", "band_0")
CORE = ("band_1",)
F32 = jnp.float32
BF16 = jnp.bfloat16
IN_VMEM = pl.BlockSpec(memory_space=pltpu.VMEM)
IN_SMEM = pl.BlockSpec(memory_space=pltpu.SMEM)
IN_ANY = pl.BlockSpec(memory_space=pl.ANY)


def shape(dims, dtype):
    return jax.ShapeDtypeStruct(dims, dtype)


def call(body, name, ins, outs, scratch=(), flops=0, moved=0, vmem=32):
    return pl.pallas_call(
        body,
        in_specs=ins,
        out_specs=jax.tree.map(lambda _: IN_VMEM, outs),
        out_shape=outs,
        scratch_shapes=list(scratch),
        compiler_params=pltpu.CompilerParams(vmem_limit_bytes=vmem * 2**20),
        cost_estimate=pl.CostEstimate(flops=flops, bytes_accessed=moved, transcendentals=0),
        name=name,
    )


def dot(a, b):
    return jnp.dot(a, b, preferred_element_type=F32)


def halves(a, axis=1):
    high = a.astype(BF16)
    return jnp.concatenate([high, (a - high.astype(F32)).astype(BF16)], axis)


def one_hot(hit):
    return jnp.where(hit, 1.0, 0.0).astype(BF16)


def scale_rows(own, width, values, mass_ref, face_ref, scaled_ref, rows_ref, picked):
    scaled_ref[:own, :] = (mass_ref[...] * values).astype(BF16).astype(F32)
    scaled_ref[own:, :] = jnp.zeros((scaled_ref.shape[0] - own, width), F32)

    def take(i, carry):
        rows = [scaled_ref[pl.ds(face_ref[0, i * 8 + u], 1), :] for u in range(8)]
        picked[pl.ds(pl.multiple_of(i * 8, 8), 8), :] = jnp.concatenate(rows, 0)
        return carry

    lax.fori_loop(0, picked.shape[0] // 8, take, 0)
    rows_ref[...] = picked[...].astype(BF16)


def start_body(face_ref, wave_ref, mass_ref, scaled_ref, rows_ref, picked):
    own, width = wave_ref.shape
    scale_rows(
        own, width, wave_ref[...].astype(F32), mass_ref, face_ref, scaled_ref, rows_ref, picked
    )


def face_hits(links_ref, own, face, cell, nodes):
    links = links_ref[:1, cell * nodes : (cell + 1) * nodes]
    return one_hot(links == lax.broadcasted_iota(jnp.int32, (face, nodes), 0) + own)


def face_matrix_body(own, face, links_ref, cells_ref, spread_ref, block_ref):
    cells, nodes, _ = cells_ref.shape
    total = jnp.zeros((face, 2 * face), F32)
    for cell in range(cells):
        hits = face_hits(links_ref, own, face, cell, nodes)
        columns = lax.dot_general(
            cells_ref[cell], hits, (((1,), (1,)), ((), ())), preferred_element_type=F32
        )
        both = halves(columns)
        spread_ref[cell * nodes : (cell + 1) * nodes, :] = both
        total = total + dot(hits, both)
    block_ref[...] = total[:, :face] + total[:, face:]


def local_body(own, face, index_ref, links_ref, scaled_ref, cells_ref, products_ref, sent_ref, held):
    cells, nodes, _ = cells_ref.shape
    width = scaled_ref.shape[1]

    def take(i, carry):
        for cell in range(cells):
            rows = [scaled_ref[pl.ds(index_ref[cell, i * 8 + u], 1), :] for u in range(8)]
            held[pl.ds(pl.multiple_of(cell * nodes + i * 8, 8), 8), :] = jnp.concatenate(rows, 0)
        return carry

    lax.fori_loop(0, nodes // 8, take, 0)
    total = jnp.zeros((face, 2 * width), F32)
    for cell in range(cells):
        part = slice(cell * nodes, (cell + 1) * nodes)
        product = dot(cells_ref[cell], held[part, :].astype(BF16))
        products_ref[part, :] = product
        total = total + dot(face_hits(links_ref, own, face, cell, nodes), halves(product))
    sent_ref[...] = total[:, :width] + total[:, width:]


def assemble_body(index_ref, products_ref, spread_ref, rows_ref, summed_ref, whole, *totals):
    cells, nodes = index_ref.shape
    own = summed_ref.shape[0]
    rows = rows_ref[...]
    twice = jnp.concatenate([rows, rows], 0)
    for cell in range(cells):
        part = slice(cell * nodes, (cell + 1) * nodes)
        whole[part, :] = products_ref[part, :] + dot(spread_ref[part, :], twice)
    for total in totals:
        total[...] = jnp.zeros_like(total)

    def add(i, carry):
        for u in range(4):
            j = i * 4 + u
            at = [pl.ds(index_ref[cell, j], 1) for cell in range(cells)]
            sums = [
                totals[cell][at[cell], :] + whole[pl.ds(cell * nodes + j, 1), :]
                for cell in range(cells)
            ]
            for cell in range(cells):
                totals[cell][at[cell], :] = sums[cell]
        return carry

    lax.fori_loop(0, nodes // 4, add, 0)

    def collect(i, carry):
        part = pl.ds(pl.multiple_of(i * 64, 64), 64)
        summed = totals[0][part, :]
        for total in totals[1:]:
            summed = summed + total[part, :]
        summed_ref[part, :] = summed
        return carry

    lax.fori_loop(0, own // 64, collect, 0)


def applied(faces_ref, summed_ref, arrived_ref, block_ref, rows_ref, mass_ref):
    own, width = summed_ref.shape
    face = rows_ref.shape[0]
    rows = rows_ref[...]
    contribution = arrived_ref[...] + dot(halves(block_ref[...]), jnp.concatenate([rows, rows], 0))
    hits = one_hot(lax.broadcasted_iota(jnp.int32, (own, face), 0) == faces_ref[:1, :])
    added = dot(hits, halves(contribution))
    return mass_ref[...] * (summed_ref[...] + (added[:, :width] + added[:, width:]))


def first_body(
    face_ref, faces_ref, summed_ref, arrived_ref, block_ref, rows_ref, mass_ref, wave_ref,
    current_ref, scaled_ref, sent_ref, picked,
):
    own, width = summed_ref.shape
    image = applied(faces_ref, summed_ref, arrived_ref, block_ref, rows_ref, mass_ref)
    current_ref[...] = (image - CENTER * wave_ref[...].astype(F32)) / HALF
    scale_rows(own, width, current_ref[...], mass_ref, face_ref, scaled_ref, sent_ref, picked)


def next_body(
    face_ref, faces_ref, summed_ref, arrived_ref, block_ref, rows_ref, mass_ref, previous_ref,
    current_ref, following_ref, scaled_ref, sent_ref, picked,
):
    own, width = summed_ref.shape
    image = applied(faces_ref, summed_ref, arrived_ref, block_ref, rows_ref, mass_ref)
    following_ref[...] = 2.0 * (image - CENTER * current_ref[...]) / HALF - previous_ref[
        ...
    ].astype(F32)
    scale_rows(own, width, following_ref[...], mass_ref, face_ref, scaled_ref, sent_ref, picked)


def last_body(
    faces_ref, summed_ref, arrived_ref, block_ref, rows_ref, mass_ref, previous_ref, current_ref,
    rounded_ref,
):
    image = applied(faces_ref, summed_ref, arrived_ref, block_ref, rows_ref, mass_ref)
    rounded_ref[...] = (
        2.0 * (image - CENTER * current_ref[...]) / HALF - previous_ref[...].astype(F32)
    ).astype(BF16)


def gram_body(rows_ref, blocks_ref):
    groups = rows_ref.shape[0]
    width = rows_ref.shape[2]
    every = jnp.concatenate([rows_ref[g] for g in range(groups)], 1)
    at = 0
    for g in range(groups):
        panel = lax.dot_general(
            rows_ref[g], every[:, g * width :], (((0,), (0,)), ((), ())),
            preferred_element_type=F32,
        )
        for h in range(groups - g):
            blocks_ref[at] = panel[:, h * width : (h + 1) * width].astype(BF16)
            at += 1


def rotate_body(nodes, band_ref, blocks_ref, every_ref, rotated_ref, gram, rows, sem):
    copy = pltpu.make_async_copy(every_ref, rows, sem)
    copy.start()
    states = gram.shape[0]
    width = rotated_ref.shape[1]
    groups = states // width
    same = lax.broadcasted_iota(jnp.int32, (width, width), 0) == lax.broadcasted_iota(
        jnp.int32, (width, width), 1
    )
    diagonal = jnp.zeros((width, width), F32)
    at = 0
    for g in range(groups):
        for h in range(g, groups):
            block = blocks_ref[at].astype(F32)
            at += 1
            gram[g * width : (g + 1) * width, h * width : (h + 1) * width] = block.astype(BF16)
            if h == g:
                diagonal = diagonal + jnp.where(same, block, 0.0)
            else:
                gram[h * width : (h + 1) * width, g * width : (g + 1) * width] = block.T.astype(
                    BF16
                )
    trace = jnp.sum(jnp.sum(diagonal, axis=0, keepdims=True), axis=1, keepdims=True)
    unit = states / trace
    first = pl.multiple_of(band_ref[0] * width, width)
    unity = (
        lax.broadcasted_iota(jnp.int32, (states, width), 0)
        == lax.broadcasted_iota(jnp.int32, (states, width), 1) + first
    ).astype(F32)

    def times_y(v):
        both = dot(gram[...], halves(v))
        return (both[:, :width] + both[:, width:]) * unit

    once = 1.5 * unity - 0.5 * (gram[:, pl.ds(first, width)].astype(F32) * unit)
    right = 1.5 * once - 0.5 * times_y(once)
    middle = times_y(right)
    product = 1.5 * middle - 0.5 * times_y(middle)
    root = 1.5 * once - 0.5 * product
    mean_eigen = trace / (states * nodes)
    both = halves(root / jnp.sqrt(mean_eigen))
    copy.wait()
    own = rotated_ref.shape[0]
    total = jnp.zeros((own, 2 * width), F32)
    for g in range(groups):
        total = total + dot(
            rows[g * own : (g + 1) * own, :], both[g * width : (g + 1) * width, :]
        )
    rotated_ref[...] = total[:, :width] + total[:, width:]


def passed_along(value, steps):
    count = lax.axis_size(DOM)
    initial, last = max(0, -steps), min(count, count - steps)
    return lax.ppermute(value, DOM, [(source, source + steps) for source in range(initial, last)])


def exchanged(pieces, axes):
    return lax.all_to_all(pieces, axes, split_axis=0, concat_axis=0, tiled=True)


def sum_of_share(array, axes):
    peers = lax.axis_size(axes)
    pieces = array.reshape(peers, array.shape[0] // peers, array.shape[1])
    return exchanged(pieces, axes).astype(F32).sum(axis=0).astype(BF16)


def shares_of_all(array, axes):
    peers = lax.axis_size(axes)
    arrived = exchanged(jnp.broadcast_to(array, (peers, *array.shape)), axes)
    return arrived.reshape(peers * array.shape[0], array.shape[1])


def on_device(wavefunctions, mass_scale, cell_matrices, connectivity, face_index):
    own, width = wavefunctions.shape
    face = face_index.shape[0]
    cells, cell_nodes = connectivity.shape
    extent = own + face
    entries = cells * cell_nodes
    domains = lax.axis_size(DOM)
    bands = lax.axis_size(BAND)

    mass = jnp.broadcast_to(mass_scale[:, None], (own, width))
    links = jnp.broadcast_to(connectivity.reshape(1, entries), (8, entries))
    faces = jnp.broadcast_to(face_index.reshape(1, face), (8, face))
    face_list = face_index.reshape(1, face)

    picked = pltpu.VMEM((face, width), F32)
    scaled_shape = shape((extent, width), F32)
    rows_shape = shape((face, width), BF16)
    wide = shape((own, width), F32)
    start = call(
        start_body, "scaled_start", [IN_SMEM] + [IN_VMEM] * 2, [scaled_shape, rows_shape], [picked],
        10**6, 3 * 2**20,
    )
    face_matrix = call(
        functools.partial(face_matrix_body, own, face), "face_matrix", [IN_VMEM] * 2,
        [shape((entries, 2 * face), BF16), shape((face, face), F32)],
        [], 3 * 10**9, 8 * 2**20,
    )
    local = call(
        functools.partial(local_body, own, face), "local_products", [IN_SMEM] + [IN_VMEM] * 3,
        [shape((entries, width), F32), shape((face, width), F32)],
        [pltpu.VMEM((entries, width), F32)], 5 * 10**9, 16 * 2**20,
    )
    assemble = call(
        assemble_body, "assembled", [IN_SMEM] + [IN_VMEM] * 3, wide,
        [pltpu.VMEM((entries, width), F32)] + [pltpu.VMEM((extent, width), F32)] * cells,
        5 * 10**9, 16 * 2**20,
    )

    scaled, rows = start(face_list, wavefunctions, mass)
    spread, block = face_matrix(links, cell_matrices)
    block = passed_along(block, 1)
    previous, current = None, wavefunctions
    for sweep in range(DEGREE):
        received = passed_along(rows, -1)
        products, sent = local(connectivity, links, scaled, cell_matrices)
        arrived = passed_along(sent, 1)
        summed = assemble(connectivity, products, spread, received)
        parts = (summed, arrived, block, rows, mass)
        if sweep == DEGREE - 1:
            rounded = call(
                last_body, "filtered", [IN_VMEM] * 8, shape((own, width), BF16), [],
                10**9, 6 * 2**20,
            )(faces, *parts, previous, current)
        elif sweep == 0:
            following, scaled, rows = call(
                first_body, "first_step", [IN_SMEM] + [IN_VMEM] * 7,
                [wide, scaled_shape, rows_shape], [picked], 10**9, 6 * 2**20,
            )(face_list, faces, *parts, current)
            previous, current = current, following
        else:
            following, scaled, rows = call(
                next_body, "next_step", [IN_SMEM] + [IN_VMEM] * 8,
                [wide, scaled_shape, rows_shape], [picked], 10**9, 6 * 2**20,
            )(face_list, faces, *parts, previous, current)
            previous, current = current, following

    every = lax.all_gather(rounded, BAND, axis=0, tiled=True)
    nodes_rows = exchanged(rounded.reshape(bands, own // bands, width), BAND)
    pairs = bands * (bands + 1) // 2
    gram = call(
        gram_body, "gram", [IN_VMEM], shape((pairs, width, width), BF16), [], 10**9, 2 * 2**20,
    )(nodes_rows)
    gram = gram.reshape(pairs * width, width)
    for axes in (CORE, PLANE, COLUMN):
        gram = sum_of_share(gram, axes)
    for axes in (COLUMN, PLANE, CORE):
        gram = shares_of_all(gram, axes)
    band = lax.axis_index(BAND).astype(jnp.int32).reshape(1)
    return call(
        functools.partial(rotate_body, own * domains), "rotated", [IN_SMEM, IN_VMEM, IN_ANY], wide,
        [
            pltpu.VMEM((bands * width, bands * width), BF16),
            pltpu.VMEM((bands * own, width), BF16),
            pltpu.SemaphoreType.DMA,
        ],
        3 * 10**9, 8 * 2**20,
    )(band, gram.reshape(pairs, width, width), every)


def solution(mesh):
    finer = Mesh(
        mesh.devices.reshape(4, 4, 2, 4, 2), ("dom_0", "dom_1", "dom_2", "band_0", "band_1")
    )
    placed = (P(DOM, BAND), P(DOM), P(DOM, None, None), P(DOM, None), P(DOM))
    return jax.shard_map(
        on_device, mesh=finer, in_specs=placed, out_specs=P(DOM, BAND), check_vma=False
    )
```

```python
import functools

import jax
import jax.numpy as jnp
from jax import lax
from jax.experimental import pallas as pl
from jax.experimental.pallas import tpu as pltpu
from jax.sharding import Mesh
from jax.sharding import PartitionSpec as P

STATES = 1024
DEGREE = 3
CENTER = 5.0
HALF = 5.0
DOM = ("dom_0", "dom_1", "dom_2")
BAND = ("band_0", "band_1")
PLANE = ("dom_0", "dom_1")
COLUMN = ("dom_2", "band_0")
CHIP = ("band_0",)
CORE = ("band_1",)
F32 = jnp.float32
BF16 = jnp.bfloat16
IN_VMEM = pl.BlockSpec(memory_space=pltpu.VMEM)
IN_SMEM = pl.BlockSpec(memory_space=pltpu.SMEM)
IN_HBM = pl.BlockSpec(memory_space=pltpu.HBM)


def shape(dims, dtype):
    return jax.ShapeDtypeStruct(dims, dtype)


def call(body, name, ins, outs, scratch=(), flops=0, moved=0, vmem=32):
    return pl.pallas_call(
        body,
        in_specs=ins,
        out_specs=jax.tree.map(lambda _: IN_VMEM, outs),
        out_shape=outs,
        scratch_shapes=list(scratch),
        compiler_params=pltpu.CompilerParams(vmem_limit_bytes=vmem * 2**20),
        cost_estimate=pl.CostEstimate(flops=flops, bytes_accessed=moved, transcendentals=0),
        name=name,
    )


def dot(a, b):
    return jnp.dot(a, b, preferred_element_type=F32)


def halves(a, axis=1):
    high = a.astype(BF16)
    return jnp.concatenate([high, (a - high.astype(F32)).astype(BF16)], axis)


def one_hot(hit):
    return jnp.where(hit, 1.0, 0.0).astype(BF16)


def scale_rows(own, width, values, mass_ref, face_ref, scaled_ref, rows_ref, picked):
    scaled_ref[:own, :] = (mass_ref[...] * values).astype(BF16).astype(F32)
    scaled_ref[own:, :] = jnp.zeros((scaled_ref.shape[0] - own, width), F32)

    def take(i, carry):
        rows = [scaled_ref[pl.ds(face_ref[0, i * 8 + u], 1), :] for u in range(8)]
        picked[pl.ds(pl.multiple_of(i * 8, 8), 8), :] = jnp.concatenate(rows, 0)
        return carry

    lax.fori_loop(0, picked.shape[0] // 8, take, 0)
    rows_ref[...] = picked[...].astype(BF16)


def start_body(face_ref, wave_ref, mass_ref, scaled_ref, rows_ref, picked):
    own, width = wave_ref.shape
    scale_rows(
        own, width, wave_ref[...].astype(F32), mass_ref, face_ref, scaled_ref, rows_ref, picked
    )


def face_hits(links_ref, own, face, cell, nodes):
    links = links_ref[:1, cell * nodes : (cell + 1) * nodes]
    return one_hot(links == lax.broadcasted_iota(jnp.int32, (face, nodes), 0) + own)


def face_matrix_body(own, face, links_ref, cells_ref, spread_ref, block_ref):
    cells, nodes, _ = cells_ref.shape
    total = jnp.zeros((face, 2 * face), F32)
    for cell in range(cells):
        hits = face_hits(links_ref, own, face, cell, nodes)
        columns = lax.dot_general(
            cells_ref[cell], hits, (((1,), (1,)), ((), ())), preferred_element_type=F32
        )
        both = halves(columns)
        spread_ref[cell * nodes : (cell + 1) * nodes, :] = both
        total = total + dot(hits, both)
    block_ref[...] = total[:, :face] + total[:, face:]


def local_body(
    own, face, index_ref, links_ref, scaled_ref, matrices_ref, products_ref, sent_ref, held,
    cells_ref, sem,
):
    copy = pltpu.make_async_copy(matrices_ref, cells_ref, sem)
    copy.start()
    cells, nodes, _ = cells_ref.shape
    width = scaled_ref.shape[1]

    def take(i, carry):
        for cell in range(cells):
            rows = [scaled_ref[pl.ds(index_ref[cell, i * 8 + u], 1), :] for u in range(8)]
            held[pl.ds(pl.multiple_of(cell * nodes + i * 8, 8), 8), :] = jnp.concatenate(rows, 0)
        return carry

    lax.fori_loop(0, nodes // 8, take, 0)
    copy.wait()
    total = jnp.zeros((face, 2 * width), F32)
    for cell in range(cells):
        part = slice(cell * nodes, (cell + 1) * nodes)
        product = dot(cells_ref[cell], held[part, :].astype(BF16))
        products_ref[part, :] = product
        total = total + dot(face_hits(links_ref, own, face, cell, nodes), halves(product))
    sent_ref[...] = total[:, :width] + total[:, width:]


def assemble_body(index_ref, products_ref, spread_ref, rows_ref, summed_ref, whole, *totals):
    cells, nodes = index_ref.shape
    own = summed_ref.shape[0]
    rows = rows_ref[...]
    twice = jnp.concatenate([rows, rows], 0)
    for cell in range(cells):
        part = slice(cell * nodes, (cell + 1) * nodes)
        whole[part, :] = products_ref[part, :] + dot(spread_ref[part, :], twice)
    for total in totals:
        total[...] = jnp.zeros_like(total)

    def add(i, carry):
        for u in range(4):
            j = i * 4 + u
            at = [pl.ds(index_ref[cell, j], 1) for cell in range(cells)]
            sums = [
                totals[cell][at[cell], :] + whole[pl.ds(cell * nodes + j, 1), :]
                for cell in range(cells)
            ]
            for cell in range(cells):
                totals[cell][at[cell], :] = sums[cell]
        return carry

    lax.fori_loop(0, nodes // 4, add, 0)

    def collect(i, carry):
        part = pl.ds(pl.multiple_of(i * 64, 64), 64)
        summed = totals[0][part, :]
        for total in totals[1:]:
            summed = summed + total[part, :]
        summed_ref[part, :] = summed
        return carry

    lax.fori_loop(0, own // 64, collect, 0)


def applied(faces_ref, summed_ref, arrived_ref, block_ref, rows_ref, mass_ref):
    own, width = summed_ref.shape
    face = rows_ref.shape[0]
    rows = rows_ref[...]
    contribution = arrived_ref[...] + dot(halves(block_ref[...]), jnp.concatenate([rows, rows], 0))
    hits = one_hot(lax.broadcasted_iota(jnp.int32, (own, face), 0) == faces_ref[:1, :])
    added = dot(hits, halves(contribution))
    return mass_ref[...] * (summed_ref[...] + (added[:, :width] + added[:, width:]))


def first_body(
    face_ref, faces_ref, summed_ref, arrived_ref, block_ref, rows_ref, mass_ref, wave_ref,
    current_ref, scaled_ref, sent_ref, picked,
):
    own, width = summed_ref.shape
    image = applied(faces_ref, summed_ref, arrived_ref, block_ref, rows_ref, mass_ref)
    current_ref[...] = (image - CENTER * wave_ref[...].astype(F32)) / HALF
    scale_rows(own, width, current_ref[...], mass_ref, face_ref, scaled_ref, sent_ref, picked)


def next_body(
    face_ref, faces_ref, summed_ref, arrived_ref, block_ref, rows_ref, mass_ref, previous_ref,
    current_ref, following_ref, scaled_ref, sent_ref, picked,
):
    own, width = summed_ref.shape
    image = applied(faces_ref, summed_ref, arrived_ref, block_ref, rows_ref, mass_ref)
    following_ref[...] = 2.0 * (image - CENTER * current_ref[...]) / HALF - previous_ref[
        ...
    ].astype(F32)
    scale_rows(own, width, following_ref[...], mass_ref, face_ref, scaled_ref, sent_ref, picked)


def last_body(
    faces_ref, summed_ref, arrived_ref, block_ref, rows_ref, mass_ref, previous_ref, current_ref,
    rounded_ref,
):
    image = applied(faces_ref, summed_ref, arrived_ref, block_ref, rows_ref, mass_ref)
    rounded_ref[...] = (
        2.0 * (image - CENTER * current_ref[...]) / HALF - previous_ref[...].astype(F32)
    ).astype(BF16)


def gram_body(core_ref, rows_ref, blocks_ref):
    cores, chips = rows_ref.shape[:2]
    width = rows_ref.shape[3]
    groups = chips * cores
    group = [rows_ref[g % cores, g // cores] for g in range(groups)]
    half = blocks_ref.shape[0]

    def blocks(first):
        at = 0
        for g in range(groups):
            wanted = [h for h in range(g, groups) if first <= at + h - g < first + half]
            if wanted:
                panel = lax.dot_general(
                    group[g], jnp.concatenate([group[h] for h in wanted], 1),
                    (((0,), (0,)), ((), ())), preferred_element_type=F32,
                )
                for i, h in enumerate(wanted):
                    blocks_ref[at + h - g - first] = panel[
                        :, i * width : (i + 1) * width
                    ].astype(BF16)
            at += groups - g

    for core in range(cores):
        pl.when(core_ref[0] == core)(functools.partial(blocks, core * half))


def rotate_body(nodes, band_ref, blocks_ref, every_ref, rotated_ref, gram, rows, sem):
    copy = pltpu.make_async_copy(every_ref, rows, sem)
    copy.start()
    states = gram.shape[0]
    width = rotated_ref.shape[1]
    groups = states // width
    same = lax.broadcasted_iota(jnp.int32, (width, width), 0) == lax.broadcasted_iota(
        jnp.int32, (width, width), 1
    )
    diagonal = jnp.zeros((width, width), F32)
    at = 0
    for g in range(groups):
        for h in range(g, groups):
            block = blocks_ref[at]
            at += 1
            gram[g * width : (g + 1) * width, h * width : (h + 1) * width] = block
            if h == g:
                diagonal = diagonal + jnp.where(same, block.astype(F32), 0.0)
            else:
                gram[h * width : (h + 1) * width, g * width : (g + 1) * width] = block.T
    trace = jnp.sum(jnp.sum(diagonal, axis=0, keepdims=True), axis=1, keepdims=True)
    unit = states / trace
    first = pl.multiple_of(band_ref[0] * width, width)
    unity = (
        lax.broadcasted_iota(jnp.int32, (states, width), 0)
        == lax.broadcasted_iota(jnp.int32, (states, width), 1) + first
    ).astype(F32)

    def times_y(v):
        both = dot(gram[...], halves(v))
        return (both[:, :width] + both[:, width:]) * unit

    once = 1.5 * unity - 0.5 * (gram[:, pl.ds(first, width)].astype(F32) * unit)
    right = 1.5 * once - 0.5 * times_y(once)
    middle = times_y(right)
    product = 1.5 * middle - 0.5 * times_y(middle)
    root = 1.5 * once - 0.5 * product
    mean_eigen = trace / (states * nodes)
    both = halves(root / jnp.sqrt(mean_eigen))
    copy.wait()
    own = rotated_ref.shape[0]
    total = jnp.zeros((own, 2 * width), F32)
    for g in range(groups):
        total = total + dot(
            rows[g * own : (g + 1) * own, :], both[g * width : (g + 1) * width, :]
        )
    rotated_ref[...] = total[:, :width] + total[:, width:]


def passed_along(value, steps):
    count = lax.axis_size(DOM)
    initial, last = max(0, -steps), min(count, count - steps)
    return lax.ppermute(value, DOM, [(source, source + steps) for source in range(initial, last)])


def exchanged(pieces, axes):
    return lax.all_to_all(pieces, axes, split_axis=0, concat_axis=0, tiled=True)


def sum_of_share(array, axes):
    peers = lax.axis_size(axes)
    pieces = array.reshape(peers, array.shape[0] // peers, array.shape[1])
    return exchanged(pieces, axes).astype(F32).sum(axis=0).astype(BF16)


def shares_of_all(array, axes):
    peers = lax.axis_size(axes)
    arrived = exchanged(jnp.broadcast_to(array, (peers, *array.shape)), axes)
    return arrived.reshape(peers * array.shape[0], array.shape[1])


def on_device(wavefunctions, mass_scale, cell_matrices, connectivity, face_index):
    own, width = wavefunctions.shape
    face = face_index.shape[0]
    cells, cell_nodes = connectivity.shape
    extent = own + face
    entries = cells * cell_nodes
    domains = lax.axis_size(DOM)
    bands = lax.axis_size(BAND)

    mass = jnp.broadcast_to(mass_scale[:, None], (own, width))
    links = jnp.broadcast_to(connectivity.reshape(1, entries), (8, entries))
    faces = jnp.broadcast_to(face_index.reshape(1, face), (8, face))
    face_list = face_index.reshape(1, face)

    picked = pltpu.VMEM((face, width), F32)
    scaled_shape = shape((extent, width), F32)
    rows_shape = shape((face, width), BF16)
    wide = shape((own, width), F32)
    start = call(
        start_body, "scaled_start", [IN_SMEM] + [IN_VMEM] * 2, [scaled_shape, rows_shape], [picked],
        10**6, 3 * 2**20,
    )
    face_matrix = call(
        functools.partial(face_matrix_body, own, face), "face_matrix", [IN_VMEM] * 2,
        [shape((entries, 2 * face), BF16), shape((face, face), F32)],
        [], 3 * 10**9, 8 * 2**20,
    )
    local = call(
        functools.partial(local_body, own, face), "local_products", [IN_SMEM] + [IN_VMEM] * 2 + [IN_HBM],
        [shape((entries, width), F32), shape((face, width), F32)],
        [
            pltpu.VMEM((entries, width), F32),
            pltpu.VMEM(cell_matrices.shape, BF16),
            pltpu.SemaphoreType.DMA,
        ],
        5 * 10**9, 16 * 2**20,
    )
    assemble = call(
        assemble_body, "assembled", [IN_SMEM] + [IN_VMEM] * 3, wide,
        [pltpu.VMEM((entries, width), F32)] + [pltpu.VMEM((extent, width), F32)] * cells,
        5 * 10**9, 16 * 2**20,
    )

    scaled, rows = start(face_list, wavefunctions, mass)
    spread, block = face_matrix(links, cell_matrices)
    block = passed_along(block, 1)
    previous, current = None, wavefunctions
    for sweep in range(DEGREE):
        received = passed_along(rows, -1)
        products, sent = local(connectivity, links, scaled, cell_matrices)
        arrived = passed_along(sent, 1)
        summed = assemble(connectivity, products, spread, received)
        parts = (summed, arrived, block, rows, mass)
        if sweep == DEGREE - 1:
            rounded = call(
                last_body, "filtered", [IN_VMEM] * 8, shape((own, width), BF16), [],
                10**9, 6 * 2**20,
            )(faces, *parts, previous, current)
        elif sweep == 0:
            following, scaled, rows = call(
                first_body, "first_step", [IN_SMEM] + [IN_VMEM] * 7,
                [wide, scaled_shape, rows_shape], [picked], 10**9, 6 * 2**20,
            )(face_list, faces, *parts, current)
            previous, current = current, following
        else:
            following, scaled, rows = call(
                next_body, "next_step", [IN_SMEM] + [IN_VMEM] * 8,
                [wide, scaled_shape, rows_shape], [picked], 10**9, 6 * 2**20,
            )(face_list, faces, *parts, previous, current)
            previous, current = current, following

    chips, cores = lax.axis_size(CHIP), lax.axis_size(CORE)
    mine = exchanged(rounded.reshape(chips, own // chips, width), CHIP)
    rounded, mine = lax.optimization_barrier((rounded, mine))
    every = lax.all_gather(rounded, BAND, axis=0, tiled=True)
    both = exchanged(jnp.broadcast_to(mine, (cores, *mine.shape)), CORE)
    pairs = bands * (bands + 1) // 2
    half = pairs // cores
    core = lax.axis_index(CORE).astype(jnp.int32).reshape(1)
    gram = call(
        gram_body, "gram", [IN_SMEM, IN_VMEM], shape((half, width, width), BF16), [],
        10**9, 3 * 2**20,
    )(core, both)
    gram = sum_of_share(gram.reshape(half * width, width), PLANE)
    columns = lax.axis_size(COLUMN)
    gram = exchanged(jnp.broadcast_to(gram, (columns, *gram.shape)), COLUMN)
    gram = gram.astype(F32).sum(axis=0).astype(BF16)
    for axes in (PLANE, CORE):
        gram = shares_of_all(gram, axes)
    band = lax.axis_index(BAND).astype(jnp.int32).reshape(1)
    return call(
        functools.partial(rotate_body, own * domains), "rotated", [IN_SMEM, IN_VMEM, IN_HBM], wide,
        [
            pltpu.VMEM((bands * width, bands * width), BF16),
            pltpu.VMEM((bands * own, width), BF16),
            pltpu.SemaphoreType.DMA,
        ],
        3 * 10**9, 8 * 2**20,
    )(band, gram.reshape(pairs, width, width), every)


def solution(mesh):
    finer = Mesh(
        mesh.devices.reshape(4, 4, 2, 4, 2), ("dom_0", "dom_1", "dom_2", "band_0", "band_1")
    )
    placed = (P(DOM, BAND), P(DOM), P(DOM, None, None), P(DOM, None), P(DOM))
    return jax.shard_map(
        on_device, mesh=finer, in_specs=placed, out_specs=P(DOM, BAND), check_vma=False
    )
```

```python
import functools

import jax
import jax.numpy as jnp
from jax import lax
from jax.experimental import pallas as pl
from jax.experimental.pallas import tpu as pltpu
from jax.sharding import Mesh
from jax.sharding import PartitionSpec as P

STATES = 1024
DEGREE = 3
CENTER = 5.0
HALF = 5.0
DOM = ("dom_0", "dom_1", "dom_2")
BAND = ("band_0", "band_1")
PLANE = ("dom_0", "dom_1")
COLUMN = ("dom_2", "band_0")
CHIP = ("band_0",)
CORE = ("band_1",)
F32 = jnp.float32
BF16 = jnp.bfloat16
IN_VMEM = pl.BlockSpec(memory_space=pltpu.VMEM)
IN_SMEM = pl.BlockSpec(memory_space=pltpu.SMEM)
IN_ANY = pl.BlockSpec(memory_space=pl.ANY)


def shape(dims, dtype):
    return jax.ShapeDtypeStruct(dims, dtype)


def call(body, name, ins, outs, scratch=(), flops=0, moved=0, vmem=32):
    return pl.pallas_call(
        body,
        in_specs=ins,
        out_specs=jax.tree.map(lambda _: IN_VMEM, outs),
        out_shape=outs,
        scratch_shapes=list(scratch),
        compiler_params=pltpu.CompilerParams(vmem_limit_bytes=vmem * 2**20),
        cost_estimate=pl.CostEstimate(flops=flops, bytes_accessed=moved, transcendentals=0),
        name=name,
    )


def dot(a, b):
    return jnp.dot(a, b, preferred_element_type=F32)


def halves(a, axis=1):
    high = a.astype(BF16)
    return jnp.concatenate([high, (a - high.astype(F32)).astype(BF16)], axis)


def one_hot(hit):
    return jnp.where(hit, 1.0, 0.0).astype(BF16)


def scale_rows(own, width, values, mass_ref, face_ref, scaled_ref, rows_ref, picked):
    scaled_ref[:own, :] = (mass_ref[...] * values).astype(BF16).astype(F32)
    scaled_ref[own:, :] = jnp.zeros((scaled_ref.shape[0] - own, width), F32)

    def take(i, carry):
        rows = [scaled_ref[pl.ds(face_ref[0, i * 8 + u], 1), :] for u in range(8)]
        picked[pl.ds(pl.multiple_of(i * 8, 8), 8), :] = jnp.concatenate(rows, 0)
        return carry

    lax.fori_loop(0, picked.shape[0] // 8, take, 0)
    rows_ref[...] = picked[...].astype(BF16)


def start_body(face_ref, wave_ref, mass_ref, scaled_ref, rows_ref, picked):
    own, width = wave_ref.shape
    scale_rows(
        own, width, wave_ref[...].astype(F32), mass_ref, face_ref, scaled_ref, rows_ref, picked
    )


def face_hits(links_ref, own, face, cell, nodes):
    links = links_ref[:1, cell * nodes : (cell + 1) * nodes]
    return one_hot(links == lax.broadcasted_iota(jnp.int32, (face, nodes), 0) + own)


def take_entries(index_ref, scaled_ref, held):
    cells, nodes = index_ref.shape

    def take(i, carry):
        for cell in range(cells):
            rows = [scaled_ref[pl.ds(index_ref[cell, i * 8 + u], 1), :] for u in range(8)]
            held[pl.ds(pl.multiple_of(cell * nodes + i * 8, 8), 8), :] = jnp.concatenate(rows, 0)
        return carry

    lax.fori_loop(0, nodes // 8, take, 0)


def opening_body(
    own, face, index_ref, links_ref, scaled_ref, matrices_ref, products_ref, spread_ref, sent_ref,
    held, cells_ref, sem,
):
    copy = pltpu.make_async_copy(matrices_ref, cells_ref, sem)
    copy.start()
    take_entries(index_ref, scaled_ref, held)
    copy.wait()
    cells, nodes = index_ref.shape
    width = scaled_ref.shape[1]
    total = jnp.zeros((face, 2 * width), F32)
    block = jnp.zeros((face, 2 * face), F32)
    for cell in range(cells):
        part = slice(cell * nodes, (cell + 1) * nodes)
        hits = face_hits(links_ref, own, face, cell, nodes)
        columns = lax.dot_general(
            cells_ref[cell], hits, (((1,), (1,)), ((), ())), preferred_element_type=F32
        )
        both = halves(columns)
        spread_ref[part, :] = both
        block = block + dot(hits, both)
        product = dot(cells_ref[cell], held[part, :].astype(BF16))
        products_ref[part, :] = product
        total = total + dot(hits, halves(product))
    sent_ref[:, :width] = total[:, :width] + total[:, width:]
    sent_ref[:, width:] = block[:, :face] + block[:, face:]


def local_body(own, face, index_ref, links_ref, scaled_ref, cells_ref, products_ref, sent_ref, held):
    take_entries(index_ref, scaled_ref, held)
    cells, nodes = index_ref.shape
    width = scaled_ref.shape[1]
    total = jnp.zeros((face, 2 * width), F32)
    for cell in range(cells):
        part = slice(cell * nodes, (cell + 1) * nodes)
        product = dot(cells_ref[cell], held[part, :].astype(BF16))
        products_ref[part, :] = product
        total = total + dot(face_hits(links_ref, own, face, cell, nodes), halves(product))
    sent_ref[...] = total[:, :width] + total[:, width:]


def assemble_body(index_ref, products_ref, spread_ref, rows_ref, summed_ref, whole, *totals):
    cells, nodes = index_ref.shape
    own = summed_ref.shape[0]
    rows = rows_ref[...]
    twice = jnp.concatenate([rows, rows], 0)
    for cell in range(cells):
        part = slice(cell * nodes, (cell + 1) * nodes)
        whole[part, :] = products_ref[part, :] + dot(spread_ref[part, :], twice)
    for total in totals:
        total[...] = jnp.zeros_like(total)

    def add(i, carry):
        for u in range(4):
            j = i * 4 + u
            at = [pl.ds(index_ref[cell, j], 1) for cell in range(cells)]
            sums = [
                totals[cell][at[cell], :] + whole[pl.ds(cell * nodes + j, 1), :]
                for cell in range(cells)
            ]
            for cell in range(cells):
                totals[cell][at[cell], :] = sums[cell]
        return carry

    lax.fori_loop(0, nodes // 4, add, 0)

    def collect(i, carry):
        part = pl.ds(pl.multiple_of(i * 64, 64), 64)
        summed = totals[0][part, :]
        for total in totals[1:]:
            summed = summed + total[part, :]
        summed_ref[part, :] = summed
        return carry

    lax.fori_loop(0, own // 64, collect, 0)


def applied(faces_ref, summed_ref, arrived_ref, block_ref, rows_ref, mass_ref):
    own, width = summed_ref.shape
    face = rows_ref.shape[0]
    rows = rows_ref[...]
    block = block_ref[:, width:]
    contribution = arrived_ref[:, :width] + dot(halves(block), jnp.concatenate([rows, rows], 0))
    hits = one_hot(lax.broadcasted_iota(jnp.int32, (own, face), 0) == faces_ref[:1, :])
    added = dot(hits, halves(contribution))
    return mass_ref[...] * (summed_ref[...] + (added[:, :width] + added[:, width:]))


def first_body(
    face_ref, faces_ref, summed_ref, arrived_ref, block_ref, rows_ref, mass_ref, wave_ref,
    current_ref, scaled_ref, sent_ref, picked,
):
    own, width = summed_ref.shape
    image = applied(faces_ref, summed_ref, arrived_ref, block_ref, rows_ref, mass_ref)
    current_ref[...] = (image - CENTER * wave_ref[...].astype(F32)) / HALF
    scale_rows(own, width, current_ref[...], mass_ref, face_ref, scaled_ref, sent_ref, picked)


def next_body(
    face_ref, faces_ref, summed_ref, arrived_ref, block_ref, rows_ref, mass_ref, previous_ref,
    current_ref, following_ref, scaled_ref, sent_ref, picked,
):
    own, width = summed_ref.shape
    image = applied(faces_ref, summed_ref, arrived_ref, block_ref, rows_ref, mass_ref)
    following_ref[...] = 2.0 * (image - CENTER * current_ref[...]) / HALF - previous_ref[
        ...
    ].astype(F32)
    scale_rows(own, width, following_ref[...], mass_ref, face_ref, scaled_ref, sent_ref, picked)


def last_body(
    faces_ref, summed_ref, arrived_ref, block_ref, rows_ref, mass_ref, previous_ref, current_ref,
    filtered_ref, rounded_ref,
):
    image = applied(faces_ref, summed_ref, arrived_ref, block_ref, rows_ref, mass_ref)
    filtered = 2.0 * (image - CENTER * current_ref[...]) / HALF - previous_ref[...].astype(F32)
    filtered_ref[...] = filtered
    rounded_ref[...] = filtered.astype(BF16)


def gram_body(core_ref, rows_ref, blocks_ref):
    cores, chips = rows_ref.shape[:2]
    width = rows_ref.shape[3]
    groups = chips * cores
    group = [rows_ref[g % cores, g // cores] for g in range(groups)]
    half = blocks_ref.shape[0]

    def blocks(first):
        at = 0
        for g in range(groups):
            wanted = [h for h in range(g, groups) if first <= at + h - g < first + half]
            if wanted:
                panel = lax.dot_general(
                    group[g], jnp.concatenate([group[h] for h in wanted], 1),
                    (((0,), (0,)), ((), ())), preferred_element_type=F32,
                )
                for i, h in enumerate(wanted):
                    blocks_ref[at + h - g - first] = panel[
                        :, i * width : (i + 1) * width
                    ].astype(BF16)
            at += groups - g

    for core in range(cores):
        pl.when(core_ref[0] == core)(functools.partial(blocks, core * half))


def correct_body(nodes, core_ref, blocks_ref, rows_ref, change_ref, scale_ref, excess, first, second):
    cores, chips, own, width = rows_ref.shape
    groups = chips * cores
    states = groups * width
    same = lax.broadcasted_iota(jnp.int32, (width, width), 0) == lax.broadcasted_iota(
        jnp.int32, (width, width), 1
    )
    places = [(g, h) for g in range(groups) for h in range(g, groups)]
    diagonal = jnp.zeros((width, width), F32)
    for at, (g, h) in enumerate(places):
        if g == h:
            diagonal = diagonal + jnp.where(same, blocks_ref[at].astype(F32), 0.0)
    trace = jnp.sum(jnp.sum(diagonal, axis=0, keepdims=True), axis=1, keepdims=True)
    unit = states / trace
    for at, (g, h) in enumerate(places):
        block = blocks_ref[at].astype(F32) * unit
        if g == h:
            block = block - same.astype(F32)
        block = block.astype(BF16)
        excess[g * width : (g + 1) * width, h * width : (h + 1) * width] = block
        if g != h:
            excess[h * width : (h + 1) * width, g * width : (g + 1) * width] = block.T
    scale = 1.0 / jnp.sqrt(trace / (states * nodes))
    scale_ref[...] = jnp.broadcast_to(scale, scale_ref.shape)

    def at_core(rows):
        starts = [pl.multiple_of((cores * p + core_ref[0]) * width, width) for p in range(chips)]
        return jnp.concatenate([excess[rows, pl.ds(s, width)] for s in starts], 1)

    tall = states // 4
    parts = [slice(i * tall, (i + 1) * tall) for i in range(4)]
    for rows in parts:
        second[rows, :] = at_core(rows)
    for rows in parts:
        square = dot(excess[rows, :], second[...])
        first[rows, :] = (0.0625 * square - 0.3125 * second[rows, :].astype(F32)).astype(BF16)
    for rows in parts:
        cube = dot(excess[rows, :], first[...]) + 0.375 * at_core(rows).astype(F32)
        second[rows, :] = cube.astype(BF16)
    for rows in parts:
        added = dot(excess[rows, :], second[...]) - 0.5 * at_core(rows).astype(F32)
        first[rows, :] = (added * scale).astype(BF16)
    for p in range(own // width):
        some = slice(p * width, (p + 1) * width)
        every = jnp.concatenate([rows_ref[g % cores, g // cores, some, :] for g in range(groups)], 1)
        change = dot(every, first[...]).astype(BF16)
        for q in range(chips):
            change_ref[q, some, :] = change[:, q * width : (q + 1) * width]


def finish_body(filtered_ref, change_ref, scale_ref, rotated_ref):
    rotated_ref[...] = filtered_ref[...] * scale_ref[:1, :] + change_ref[...].astype(F32)


def passed_along(value, steps):
    count = lax.axis_size(DOM)
    initial, last = max(0, -steps), min(count, count - steps)
    return lax.ppermute(value, DOM, [(source, source + steps) for source in range(initial, last)])


def exchanged(pieces, axes):
    return lax.all_to_all(pieces, axes, split_axis=0, concat_axis=0, tiled=True)


def sum_of_share(array, axes):
    peers = lax.axis_size(axes)
    pieces = array.reshape(peers, array.shape[0] // peers, array.shape[1])
    return exchanged(pieces, axes).astype(F32).sum(axis=0).astype(BF16)


def shares_of_all(array, axes):
    peers = lax.axis_size(axes)
    arrived = exchanged(jnp.broadcast_to(array, (peers, *array.shape)), axes)
    return arrived.reshape(peers * array.shape[0], array.shape[1])


def on_device(wavefunctions, mass_scale, cell_matrices, connectivity, face_index):
    own, width = wavefunctions.shape
    face = face_index.shape[0]
    cells, cell_nodes = connectivity.shape
    extent = own + face
    entries = cells * cell_nodes
    domains = lax.axis_size(DOM)
    bands = lax.axis_size(BAND)

    mass = jnp.broadcast_to(mass_scale[:, None], (own, width))
    links = jnp.broadcast_to(connectivity.reshape(1, entries), (8, entries))
    faces = jnp.broadcast_to(face_index.reshape(1, face), (8, face))
    face_list = face_index.reshape(1, face)

    picked = pltpu.VMEM((face, width), F32)
    scaled_shape = shape((extent, width), F32)
    rows_shape = shape((face, width), BF16)
    wide = shape((own, width), F32)
    start = call(
        start_body, "scaled_start", [IN_SMEM] + [IN_VMEM] * 2, [scaled_shape, rows_shape], [picked],
        10**6, 3 * 2**20,
    )
    opening = call(
        functools.partial(opening_body, own, face), "opening_products",
        [IN_SMEM] + [IN_VMEM] * 2 + [IN_ANY],
        [
            shape((entries, width), F32), shape((entries, 2 * face), BF16),
            shape((face, width + face), F32),
        ],
        [
            pltpu.VMEM((entries, width), F32),
            pltpu.VMEM(cell_matrices.shape, BF16),
            pltpu.SemaphoreType.DMA,
        ],
        8 * 10**9, 16 * 2**20, 46,
    )
    local = call(
        functools.partial(local_body, own, face), "local_products", [IN_SMEM] + [IN_VMEM] * 3,
        [shape((entries, width), F32), shape((face, width), F32)],
        [pltpu.VMEM((entries, width), F32)], 5 * 10**9, 16 * 2**20,
    )
    assemble = call(
        assemble_body, "assembled", [IN_SMEM] + [IN_VMEM] * 3, wide,
        [pltpu.VMEM((entries, width), F32)] + [pltpu.VMEM((extent, width), F32)] * cells,
        5 * 10**9, 16 * 2**20,
    )

    scaled, rows = start(face_list, wavefunctions, mass)
    previous, current = None, wavefunctions
    for sweep in range(DEGREE):
        received = passed_along(rows, -1)
        if sweep == 0:
            products, spread, sent = opening(connectivity, links, scaled, cell_matrices)
            arrived = block = passed_along(sent, 1)
        else:
            products, sent = local(connectivity, links, scaled, cell_matrices)
            arrived = passed_along(sent, 1)
        summed = assemble(connectivity, products, spread, received)
        parts = (summed, arrived, block, rows, mass)
        if sweep == DEGREE - 1:
            filtered, rounded = call(
                last_body, "filtered", [IN_VMEM] * 8, [wide, shape((own, width), BF16)], [],
                10**9, 6 * 2**20,
            )(faces, *parts, previous, current)
        elif sweep == 0:
            following, scaled, rows = call(
                first_body, "first_step", [IN_SMEM] + [IN_VMEM] * 7,
                [wide, scaled_shape, rows_shape], [picked], 10**9, 6 * 2**20,
            )(face_list, faces, *parts, current)
            previous, current = current, following
        else:
            following, scaled, rows = call(
                next_body, "next_step", [IN_SMEM] + [IN_VMEM] * 8,
                [wide, scaled_shape, rows_shape], [picked], 10**9, 6 * 2**20,
            )(face_list, faces, *parts, previous, current)
            previous, current = current, following

    chips, cores = lax.axis_size(CHIP), lax.axis_size(CORE)
    mine = exchanged(rounded.reshape(chips, own // chips, width), CHIP)
    both = exchanged(jnp.broadcast_to(mine, (cores, *mine.shape)), CORE)
    pairs = bands * (bands + 1) // 2
    half = pairs // cores
    core = lax.axis_index(CORE).astype(jnp.int32).reshape(1)
    gram = call(
        gram_body, "gram", [IN_SMEM, IN_VMEM], shape((half, width, width), BF16), [],
        10**9, 3 * 2**20,
    )(core, both)
    gram = sum_of_share(gram.reshape(half * width, width), PLANE)
    columns = lax.axis_size(COLUMN)
    gram = exchanged(jnp.broadcast_to(gram, (columns, *gram.shape)), COLUMN)
    gram = gram.astype(F32).sum(axis=0).astype(BF16)
    for axes in (PLANE, CORE):
        gram = shares_of_all(gram, axes)
    states = bands * width
    change, scale = call(
        functools.partial(correct_body, own * domains), "correction", [IN_SMEM, IN_VMEM, IN_VMEM],
        [shape(mine.shape, BF16), shape((8, width), F32)],
        [
            pltpu.VMEM((states, states), BF16),
            pltpu.VMEM((states, chips * width), BF16),
            pltpu.VMEM((states, chips * width), BF16),
        ],
        4 * 10**9, 8 * 2**20,
    )(core, gram.reshape(pairs, width, width), both)
    change = exchanged(change, CHIP).reshape(own, width)
    return call(finish_body, "rotated", [IN_VMEM] * 3, wide, [], 10**6, 3 * 2**20)(
        filtered, change, scale
    )


def solution(mesh):
    finer = Mesh(
        mesh.devices.reshape(4, 4, 2, 4, 2), ("dom_0", "dom_1", "dom_2", "band_0", "band_1")
    )
    placed = (P(DOM, BAND), P(DOM), P(DOM, None, None), P(DOM, None), P(DOM))
    return jax.shard_map(
        on_device, mesh=finer, in_specs=placed, out_specs=P(DOM, BAND), check_vma=False
    )
```

```python
import functools

import jax
import jax.numpy as jnp
from jax import lax
from jax.experimental import pallas as pl
from jax.experimental.pallas import tpu as pltpu
from jax.sharding import Mesh
from jax.sharding import PartitionSpec as P

STATES = 1024
DEGREE = 3
CENTER = 5.0
HALF = 5.0
DOM = ("dom_0", "dom_1", "dom_2")
BAND = ("band_0", "band_1")
PLANE = ("dom_0", "dom_1")
COLUMN = ("dom_2", "band_0")
CHIP = ("band_0",)
CORE = ("band_1",)
F32 = jnp.float32
BF16 = jnp.bfloat16
IN_VMEM = pl.BlockSpec(memory_space=pltpu.VMEM)
IN_SMEM = pl.BlockSpec(memory_space=pltpu.SMEM)
IN_ANY = pl.BlockSpec(memory_space=pl.ANY)


def shape(dims, dtype):
    return jax.ShapeDtypeStruct(dims, dtype)


def call(body, name, ins, outs, scratch=(), flops=0, moved=0, vmem=32):
    return pl.pallas_call(
        body,
        in_specs=ins,
        out_specs=jax.tree.map(lambda _: IN_VMEM, outs),
        out_shape=outs,
        scratch_shapes=list(scratch),
        compiler_params=pltpu.CompilerParams(vmem_limit_bytes=vmem * 2**20),
        cost_estimate=pl.CostEstimate(flops=flops, bytes_accessed=moved, transcendentals=0),
        name=name,
    )


def dot(a, b):
    return jnp.dot(a, b, preferred_element_type=F32)


def halves(a, axis=1):
    high = a.astype(BF16)
    return jnp.concatenate([high, (a - high.astype(F32)).astype(BF16)], axis)


def one_hot(hit):
    return jnp.where(hit, 1.0, 0.0).astype(BF16)


def scale_rows(own, width, values, mass_ref, face_ref, scaled_ref, rows_ref, picked):
    scaled_ref[:own, :] = (mass_ref[...] * values).astype(BF16).astype(F32)
    scaled_ref[own:, :] = jnp.zeros((scaled_ref.shape[0] - own, width), F32)

    def take(i, carry):
        rows = [scaled_ref[pl.ds(face_ref[0, i * 8 + u], 1), :] for u in range(8)]
        picked[pl.ds(pl.multiple_of(i * 8, 8), 8), :] = jnp.concatenate(rows, 0)
        return carry

    lax.fori_loop(0, picked.shape[0] // 8, take, 0)
    rows_ref[...] = picked[...].astype(BF16)


def start_body(face_ref, wave_ref, mass_ref, scaled_ref, rows_ref, picked):
    own, width = wave_ref.shape
    scale_rows(
        own, width, wave_ref[...].astype(F32), mass_ref, face_ref, scaled_ref, rows_ref, picked
    )


def face_hits(links_ref, own, face, cell, nodes):
    links = links_ref[:1, cell * nodes : (cell + 1) * nodes]
    return one_hot(links == lax.broadcasted_iota(jnp.int32, (face, nodes), 0) + own)


def take_entries(index_ref, column_ref, scaled_ref, held, narrow):
    cells, nodes = index_ref.shape
    extent, width = scaled_ref.shape
    copied = cells - column_ref.shape[0] // nodes
    narrow[...] = scaled_ref[...].astype(BF16)
    steps = 4
    some = nodes // steps
    rest = column_ref.shape[0] // steps

    def take(i, carry):
        first = pl.multiple_of(i * rest, rest)
        named = column_ref[pl.ds(first, rest), :]
        lane = lax.broadcasted_iota(jnp.int32, (rest, 128), 1)
        hits = jnp.concatenate([one_hot(named == lane + t) for t in range(0, extent, 128)], 1)
        product = dot(hits, narrow[...])
        for k in range(some // 8):
            for cell in range(copied):
                at = i * some + k * 8
                rows = [scaled_ref[pl.ds(index_ref[cell, at + u], 1), :] for u in range(8)]
                held[pl.ds(pl.multiple_of(cell * nodes + at, 8), 8), :] = jnp.concatenate(rows, 0)
        held[pl.ds(copied * nodes + first, rest), :] = product
        return carry

    lax.fori_loop(0, steps, take, 0)


def opening_body(
    own, face, index_ref, links_ref, column_ref, scaled_ref, matrices_ref, products_ref,
    spread_ref, block_ref, sent_ref, held, narrow, cells_ref, sem,
):
    copy = pltpu.make_async_copy(matrices_ref, cells_ref, sem)
    copy.start()
    take_entries(index_ref, column_ref, scaled_ref, held, narrow)
    copy.wait()
    cells, nodes = index_ref.shape
    width = scaled_ref.shape[1]
    total = jnp.zeros((face, 2 * width), F32)
    block = jnp.zeros((face, 2 * face), F32)
    for cell in range(cells):
        part = slice(cell * nodes, (cell + 1) * nodes)
        hits = face_hits(links_ref, own, face, cell, nodes)
        columns = lax.dot_general(
            cells_ref[cell], hits, (((1,), (1,)), ((), ())), preferred_element_type=F32
        )
        both = halves(columns)
        spread_ref[part, :] = both
        block = block + dot(hits, both)
        product = dot(cells_ref[cell], held[part, :].astype(BF16))
        products_ref[part, :] = product
        total = total + dot(hits, halves(product))
    sent_ref[...] = total[:, :width] + total[:, width:]
    block_ref[...] = halves(block[:, :face] + block[:, face:])


def local_body(
    own, face, index_ref, links_ref, column_ref, scaled_ref, cells_ref, products_ref, sent_ref,
    held, narrow,
):
    take_entries(index_ref, column_ref, scaled_ref, held, narrow)
    cells, nodes = index_ref.shape
    width = scaled_ref.shape[1]
    total = jnp.zeros((face, 2 * width), F32)
    for cell in range(cells):
        part = slice(cell * nodes, (cell + 1) * nodes)
        product = dot(cells_ref[cell], held[part, :].astype(BF16))
        products_ref[part, :] = product
        total = total + dot(face_hits(links_ref, own, face, cell, nodes), halves(product))
    sent_ref[...] = total[:, :width] + total[:, width:]


def returned_body(sent_ref, block_ref, rows_ref, total_ref):
    rows = rows_ref[...]
    total_ref[...] = sent_ref[...] + dot(block_ref[...], jnp.concatenate([rows, rows], 0))


def assemble_body(
    index_ref, links_ref, products_ref, spread_ref, rows_ref, summed_ref, whole, split, *totals
):
    cells, nodes = index_ref.shape
    own, width = summed_ref.shape
    added = len(totals)
    rows = rows_ref[...]
    twice = jnp.concatenate([rows, rows], 0)
    for cell in range(cells):
        part = slice(cell * nodes, (cell + 1) * nodes)
        product = products_ref[part, :] + dot(spread_ref[part, :], twice)
        if cell < added:
            whole[part, :] = product
        else:
            split[(cell - added) * nodes : (cell - added + 1) * nodes, :] = halves(product)
    for total in totals:
        total[...] = jnp.zeros_like(total)
    steps = 4
    some = nodes // steps
    tall = own // steps

    def add(i, carry):
        first = pl.multiple_of(i * tall, tall)
        row = lax.broadcasted_iota(jnp.int32, (tall, 128), 0) + first
        hits = jnp.concatenate(
            [
                one_hot(links_ref[:1, t : t + 128] == row)
                for t in range(added * nodes, cells * nodes, 128)
            ],
            1,
        )
        both = dot(hits, split[...])
        for u in range(some):
            j = i * some + u
            at = [pl.ds(index_ref[cell, j], 1) for cell in range(added)]
            sums = [
                totals[cell][at[cell], :] + whole[pl.ds(cell * nodes + j, 1), :]
                for cell in range(added)
            ]
            for cell in range(added):
                totals[cell][at[cell], :] = sums[cell]
        summed_ref[pl.ds(first, tall), :] = both[:, :width] + both[:, width:]
        return carry

    lax.fori_loop(0, steps, add, 0)

    def collect(i, carry):
        part = pl.ds(pl.multiple_of(i * 64, 64), 64)
        summed = summed_ref[part, :]
        for total in totals:
            summed = summed + total[part, :]
        summed_ref[part, :] = summed
        return carry

    lax.fori_loop(0, own // 64, collect, 0)


def applied(faces_ref, summed_ref, arrived_ref, mass_ref):
    own, width = summed_ref.shape
    face = arrived_ref.shape[0]
    hits = one_hot(lax.broadcasted_iota(jnp.int32, (own, face), 0) == faces_ref[:1, :])
    added = dot(hits, halves(arrived_ref[...]))
    return mass_ref[...] * (summed_ref[...] + (added[:, :width] + added[:, width:]))


def first_body(
    face_ref, faces_ref, summed_ref, arrived_ref, mass_ref, wave_ref,
    current_ref, scaled_ref, sent_ref, picked,
):
    own, width = summed_ref.shape
    image = applied(faces_ref, summed_ref, arrived_ref, mass_ref)
    current_ref[...] = (image - CENTER * wave_ref[...].astype(F32)) / HALF
    scale_rows(own, width, current_ref[...], mass_ref, face_ref, scaled_ref, sent_ref, picked)


def next_body(
    face_ref, faces_ref, summed_ref, arrived_ref, mass_ref, previous_ref,
    current_ref, following_ref, scaled_ref, sent_ref, picked,
):
    own, width = summed_ref.shape
    image = applied(faces_ref, summed_ref, arrived_ref, mass_ref)
    following_ref[...] = 2.0 * (image - CENTER * current_ref[...]) / HALF - previous_ref[
        ...
    ].astype(F32)
    scale_rows(own, width, following_ref[...], mass_ref, face_ref, scaled_ref, sent_ref, picked)


def last_body(
    faces_ref, summed_ref, arrived_ref, mass_ref, previous_ref, current_ref,
    filtered_ref, rounded_ref,
):
    image = applied(faces_ref, summed_ref, arrived_ref, mass_ref)
    filtered = 2.0 * (image - CENTER * current_ref[...]) / HALF - previous_ref[...].astype(F32)
    filtered_ref[...] = filtered
    rounded_ref[...] = filtered.astype(BF16)


def gram_body(core_ref, rows_ref, blocks_ref):
    cores, chips = rows_ref.shape[:2]
    width = rows_ref.shape[3]
    groups = chips * cores
    group = [rows_ref[g % cores, g // cores] for g in range(groups)]
    half = blocks_ref.shape[0]

    def blocks(first):
        at = 0
        for g in range(groups):
            wanted = [h for h in range(g, groups) if first <= at + h - g < first + half]
            if wanted:
                panel = lax.dot_general(
                    group[g], jnp.concatenate([group[h] for h in wanted], 1),
                    (((0,), (0,)), ((), ())), preferred_element_type=F32,
                )
                for i, h in enumerate(wanted):
                    blocks_ref[at + h - g - first] = panel[
                        :, i * width : (i + 1) * width
                    ].astype(BF16)
            at += groups - g

    for core in range(cores):
        pl.when(core_ref[0] == core)(functools.partial(blocks, core * half))


def correct_body(nodes, core_ref, blocks_ref, rows_ref, change_ref, scale_ref, excess, first, second):
    cores, chips, own, width = rows_ref.shape
    groups = chips * cores
    states = groups * width
    same = lax.broadcasted_iota(jnp.int32, (width, width), 0) == lax.broadcasted_iota(
        jnp.int32, (width, width), 1
    )
    places = [(g, h) for g in range(groups) for h in range(g, groups)]
    diagonal = jnp.zeros((width, width), F32)
    for at, (g, h) in enumerate(places):
        if g == h:
            diagonal = diagonal + jnp.where(same, blocks_ref[at].astype(F32), 0.0)
    trace = jnp.sum(jnp.sum(diagonal, axis=0, keepdims=True), axis=1, keepdims=True)
    unit = states / trace
    for at, (g, h) in enumerate(places):
        block = blocks_ref[at].astype(F32) * unit
        if g == h:
            block = block - same.astype(F32)
        block = block.astype(BF16)
        excess[g * width : (g + 1) * width, h * width : (h + 1) * width] = block
        if g != h:
            excess[h * width : (h + 1) * width, g * width : (g + 1) * width] = block.T
    scale = 1.0 / jnp.sqrt(trace / (states * nodes))
    scale_ref[...] = jnp.broadcast_to(scale, scale_ref.shape)

    def at_core(rows):
        starts = [pl.multiple_of((cores * p + core_ref[0]) * width, width) for p in range(chips)]
        return jnp.concatenate([excess[rows, pl.ds(s, width)] for s in starts], 1)

    tall = states // 4
    parts = [slice(i * tall, (i + 1) * tall) for i in range(4)]
    for rows in parts:
        second[rows, :] = at_core(rows)
    for rows in parts:
        square = dot(excess[rows, :], second[...])
        first[rows, :] = (0.0625 * square - 0.3125 * second[rows, :].astype(F32)).astype(BF16)
    for rows in parts:
        cube = dot(excess[rows, :], first[...]) + 0.375 * at_core(rows).astype(F32)
        second[rows, :] = cube.astype(BF16)
    for rows in parts:
        added = dot(excess[rows, :], second[...]) - 0.5 * at_core(rows).astype(F32)
        first[rows, :] = (added * scale).astype(BF16)
    for p in range(own // width):
        some = slice(p * width, (p + 1) * width)
        every = jnp.concatenate([rows_ref[g % cores, g // cores, some, :] for g in range(groups)], 1)
        change = dot(every, first[...]).astype(BF16)
        for q in range(chips):
            change_ref[q, some, :] = change[:, q * width : (q + 1) * width]


def finish_body(filtered_ref, change_ref, scale_ref, rotated_ref):
    rotated_ref[...] = filtered_ref[...] * scale_ref[:1, :] + change_ref[...].astype(F32)


def passed_along(value, steps):
    count = lax.axis_size(DOM)
    initial, last = max(0, -steps), min(count, count - steps)
    return lax.ppermute(value, DOM, [(source, source + steps) for source in range(initial, last)])


def exchanged(pieces, axes):
    return lax.all_to_all(pieces, axes, split_axis=0, concat_axis=0, tiled=True)


def sum_of_share(array, axes):
    peers = lax.axis_size(axes)
    pieces = array.reshape(peers, array.shape[0] // peers, array.shape[1])
    return exchanged(pieces, axes).astype(F32).sum(axis=0).astype(BF16)


def shares_of_all(array, axes):
    peers = lax.axis_size(axes)
    arrived = exchanged(jnp.broadcast_to(array, (peers, *array.shape)), axes)
    return arrived.reshape(peers * array.shape[0], array.shape[1])


def on_device(wavefunctions, mass_scale, cell_matrices, connectivity, face_index):
    own, width = wavefunctions.shape
    face = face_index.shape[0]
    cells, cell_nodes = connectivity.shape
    extent = own + face
    entries = cells * cell_nodes
    domains = lax.axis_size(DOM)
    bands = lax.axis_size(BAND)

    mass = jnp.broadcast_to(mass_scale[:, None], (own, width))
    links = jnp.broadcast_to(connectivity.reshape(1, entries), (8, entries))
    copied = cells // 2
    column = jnp.broadcast_to(
        connectivity[copied:].reshape(-1, 1), ((cells - copied) * cell_nodes, 128)
    )
    faces = jnp.broadcast_to(face_index.reshape(1, face), (8, face))
    face_list = face_index.reshape(1, face)

    picked = pltpu.VMEM((face, width), F32)
    scaled_shape = shape((extent, width), F32)
    rows_shape = shape((face, width), BF16)
    wide = shape((own, width), F32)
    start = call(
        start_body, "scaled_start", [IN_SMEM] + [IN_VMEM] * 2, [scaled_shape, rows_shape], [picked],
        10**6, 3 * 2**20,
    )
    gathering = [pltpu.VMEM((entries, width), F32), pltpu.VMEM((extent, width), BF16)]
    opening = call(
        functools.partial(opening_body, own, face), "opening_products",
        [IN_SMEM] + [IN_VMEM] * 3 + [IN_ANY],
        [
            shape((entries, width), F32), shape((entries, 2 * face), BF16),
            shape((face, 2 * face), BF16), shape((face, width), F32),
        ],
        gathering + [pltpu.VMEM(cell_matrices.shape, BF16), pltpu.SemaphoreType.DMA],
        8 * 10**9, 16 * 2**20, 45,
    )
    local = call(
        functools.partial(local_body, own, face), "local_products", [IN_SMEM] + [IN_VMEM] * 4,
        [shape((entries, width), F32), shape((face, width), F32)], gathering,
        5 * 10**9, 16 * 2**20,
    )
    returned = call(
        returned_body, "returned", [IN_VMEM] * 3, shape((face, width), F32), [], 10**8, 2**20,
    )
    assemble = call(
        assemble_body, "assembled", [IN_SMEM] + [IN_VMEM] * 4, wide,
        [
            pltpu.VMEM((copied * cell_nodes, width), F32),
            pltpu.VMEM((entries - copied * cell_nodes, 2 * width), BF16),
        ]
        + [pltpu.VMEM((extent, width), F32)] * copied,
        5 * 10**9, 16 * 2**20,
    )

    scaled, rows = start(face_list, wavefunctions, mass)
    previous, current = None, wavefunctions
    for sweep in range(DEGREE):
        received = passed_along(rows, -1)
        if sweep == 0:
            products, spread, block, sent = opening(
                connectivity, links, column, scaled, cell_matrices
            )
        else:
            products, sent = local(connectivity, links, column, scaled, cell_matrices)
        arrived = passed_along(returned(sent, block, received), 1)
        summed = assemble(connectivity, links, products, spread, received)
        parts = (summed, arrived, mass)
        if sweep == DEGREE - 1:
            filtered, rounded = call(
                last_body, "filtered", [IN_VMEM] * 6, [wide, shape((own, width), BF16)], [],
                10**9, 6 * 2**20,
            )(faces, *parts, previous, current)
        elif sweep == 0:
            following, scaled, rows = call(
                first_body, "first_step", [IN_SMEM] + [IN_VMEM] * 5,
                [wide, scaled_shape, rows_shape], [picked], 10**9, 6 * 2**20,
            )(face_list, faces, *parts, current)
            previous, current = current, following
        else:
            following, scaled, rows = call(
                next_body, "next_step", [IN_SMEM] + [IN_VMEM] * 6,
                [wide, scaled_shape, rows_shape], [picked], 10**9, 6 * 2**20,
            )(face_list, faces, *parts, previous, current)
            previous, current = current, following

    chips, cores = lax.axis_size(CHIP), lax.axis_size(CORE)
    mine = exchanged(rounded.reshape(chips, own // chips, width), CHIP)
    both = exchanged(jnp.broadcast_to(mine, (cores, *mine.shape)), CORE)
    pairs = bands * (bands + 1) // 2
    half = pairs // cores
    core = lax.axis_index(CORE).astype(jnp.int32).reshape(1)
    gram = call(
        gram_body, "gram", [IN_SMEM, IN_VMEM], shape((half, width, width), BF16), [],
        10**9, 3 * 2**20,
    )(core, both)
    gram = sum_of_share(gram.reshape(half * width, width), PLANE)
    columns = lax.axis_size(COLUMN)
    gram = exchanged(jnp.broadcast_to(gram, (columns, *gram.shape)), COLUMN)
    gram = gram.astype(F32).sum(axis=0).astype(BF16)
    for axes in (PLANE, CORE):
        gram = shares_of_all(gram, axes)
    states = bands * width
    change, scale = call(
        functools.partial(correct_body, own * domains), "correction", [IN_SMEM, IN_VMEM, IN_VMEM],
        [shape(mine.shape, BF16), shape((8, width), F32)],
        [
            pltpu.VMEM((states, states), BF16),
            pltpu.VMEM((states, chips * width), BF16),
            pltpu.VMEM((states, chips * width), BF16),
        ],
        4 * 10**9, 8 * 2**20,
    )(core, gram.reshape(pairs, width, width), both)
    change = exchanged(change, CHIP).reshape(own, width)
    return call(finish_body, "rotated", [IN_VMEM] * 3, wide, [], 10**6, 3 * 2**20)(
        filtered, change, scale
    )


def solution(mesh):
    finer = Mesh(
        mesh.devices.reshape(4, 4, 2, 4, 2), ("dom_0", "dom_1", "dom_2", "band_0", "band_1")
    )
    placed = (P(DOM, BAND), P(DOM), P(DOM, None, None), P(DOM, None), P(DOM))
    return jax.shard_map(
        on_device, mesh=finer, in_specs=placed, out_specs=P(DOM, BAND), check_vma=False
    )
```

```python
import functools

import jax
import jax.numpy as jnp
from jax import lax
from jax.experimental import pallas as pl
from jax.experimental.pallas import tpu as pltpu
from jax.sharding import Mesh
from jax.sharding import PartitionSpec as P

STATES = 1024
DEGREE = 3
CENTER = 5.0
HALF = 5.0
DOM = ("dom_0", "dom_1", "dom_2")
BAND = ("band_0", "band_1")
PLANE = ("dom_0", "dom_1")
COLUMN = ("dom_2", "band_0")
CHIP = ("band_0",)
CORE = ("band_1",)
F32 = jnp.float32
BF16 = jnp.bfloat16
IN_VMEM = pl.BlockSpec(memory_space=pltpu.VMEM)
IN_SMEM = pl.BlockSpec(memory_space=pltpu.SMEM)
IN_ANY = pl.BlockSpec(memory_space=pl.ANY)


def shape(dims, dtype):
    return jax.ShapeDtypeStruct(dims, dtype)


def call(body, name, ins, outs, scratch=(), flops=0, moved=0, vmem=32):
    return pl.pallas_call(
        body,
        in_specs=ins,
        out_specs=jax.tree.map(lambda _: IN_VMEM, outs),
        out_shape=outs,
        scratch_shapes=list(scratch),
        compiler_params=pltpu.CompilerParams(vmem_limit_bytes=vmem * 2**20),
        cost_estimate=pl.CostEstimate(flops=flops, bytes_accessed=moved, transcendentals=0),
        name=name,
    )


def dot(a, b):
    return jnp.dot(a, b, preferred_element_type=F32)


def halves(a, axis=1):
    high = a.astype(BF16)
    return jnp.concatenate([high, (a - high.astype(F32)).astype(BF16)], axis)


def one_hot(hit):
    return jnp.where(hit, 1.0, 0.0).astype(BF16)


def scale_rows(own, width, values, mass_ref, face_ref, scaled_ref, rows_ref, picked):
    scaled_ref[:own, :] = (mass_ref[...] * values).astype(BF16).astype(F32)
    scaled_ref[own:, :] = jnp.zeros((scaled_ref.shape[0] - own, width), F32)

    def take(i, carry):
        rows = [scaled_ref[pl.ds(face_ref[0, i * 8 + u], 1), :] for u in range(8)]
        picked[pl.ds(pl.multiple_of(i * 8, 8), 8), :] = jnp.concatenate(rows, 0)
        return carry

    lax.fori_loop(0, picked.shape[0] // 8, take, 0)
    rows_ref[...] = picked[...].astype(BF16)


def start_body(face_ref, wave_ref, mass_ref, scaled_ref, rows_ref, picked):
    own, width = wave_ref.shape
    scale_rows(
        own, width, wave_ref[...].astype(F32), mass_ref, face_ref, scaled_ref, rows_ref, picked
    )


def face_hits(links_ref, own, face, cell, nodes):
    links = links_ref[:1, cell * nodes : (cell + 1) * nodes]
    return one_hot(links == lax.broadcasted_iota(jnp.int32, (face, nodes), 0) + own)


def take_entries(index_ref, column_ref, scaled_ref, held, narrow):
    cells, nodes = index_ref.shape
    extent, width = scaled_ref.shape
    copied = cells - column_ref.shape[0] // nodes
    narrow[...] = scaled_ref[...].astype(BF16)
    steps = 4
    some = nodes // steps
    rest = column_ref.shape[0] // steps

    def take(i, carry):
        first = pl.multiple_of(i * rest, rest)
        named = column_ref[pl.ds(first, rest), :]
        lane = lax.broadcasted_iota(jnp.int32, (rest, 128), 1)
        hits = jnp.concatenate([one_hot(named == lane + t) for t in range(0, extent, 128)], 1)
        product = dot(hits, narrow[...])
        for k in range(some // 8):
            for cell in range(copied):
                at = i * some + k * 8
                rows = [scaled_ref[pl.ds(index_ref[cell, at + u], 1), :] for u in range(8)]
                held[pl.ds(pl.multiple_of(cell * nodes + at, 8), 8), :] = jnp.concatenate(rows, 0)
        held[pl.ds(copied * nodes + first, rest), :] = product
        return carry

    lax.fori_loop(0, steps, take, 0)


def opening_body(
    own, face, index_ref, links_ref, column_ref, scaled_ref, matrices_ref, products_ref,
    spread_ref, block_ref, sent_ref, held, narrow, cells_ref, sem,
):
    copy = pltpu.make_async_copy(matrices_ref, cells_ref, sem)
    copy.start()
    take_entries(index_ref, column_ref, scaled_ref, held, narrow)
    copy.wait()
    cells, nodes = index_ref.shape
    width = scaled_ref.shape[1]
    total = jnp.zeros((face, 2 * width), F32)
    block = jnp.zeros((face, 2 * face), F32)
    for cell in range(cells):
        part = slice(cell * nodes, (cell + 1) * nodes)
        hits = face_hits(links_ref, own, face, cell, nodes)
        columns = lax.dot_general(
            cells_ref[cell], hits, (((1,), (1,)), ((), ())), preferred_element_type=F32
        )
        both = halves(columns)
        spread_ref[part, :] = both
        block = block + dot(hits, both)
        product = dot(cells_ref[cell], held[part, :].astype(BF16))
        products_ref[part, :] = product
        total = total + dot(hits, halves(product))
    sent_ref[...] = total[:, :width] + total[:, width:]
    block_ref[...] = halves(block[:, :face] + block[:, face:])


def local_body(
    own, face, index_ref, links_ref, column_ref, scaled_ref, cells_ref, products_ref, sent_ref,
    held, narrow,
):
    take_entries(index_ref, column_ref, scaled_ref, held, narrow)
    cells, nodes = index_ref.shape
    width = scaled_ref.shape[1]
    total = jnp.zeros((face, 2 * width), F32)
    for cell in range(cells):
        part = slice(cell * nodes, (cell + 1) * nodes)
        product = dot(cells_ref[cell], held[part, :].astype(BF16))
        products_ref[part, :] = product
        total = total + dot(face_hits(links_ref, own, face, cell, nodes), halves(product))
    sent_ref[...] = total[:, :width] + total[:, width:]


def returned_body(sent_ref, block_ref, rows_ref, total_ref):
    rows = rows_ref[...]
    total = sent_ref[...] + dot(block_ref[...], jnp.concatenate([rows, rows], 0))
    total_ref[...] = total.astype(BF16)


def assemble_body(
    index_ref, links_ref, products_ref, spread_ref, rows_ref, summed_ref, whole, split, *totals
):
    cells, nodes = index_ref.shape
    own, width = summed_ref.shape
    added = len(totals)
    rows = rows_ref[...]
    twice = jnp.concatenate([rows, rows], 0)
    for cell in range(cells):
        part = slice(cell * nodes, (cell + 1) * nodes)
        product = products_ref[part, :] + dot(spread_ref[part, :], twice)
        if cell < added:
            whole[part, :] = product
        else:
            split[(cell - added) * nodes : (cell - added + 1) * nodes, :] = halves(product)
    for total in totals:
        total[...] = jnp.zeros_like(total)
    steps = 4
    some = nodes // steps
    tall = own // steps

    def add(i, carry):
        first = pl.multiple_of(i * tall, tall)
        row = lax.broadcasted_iota(jnp.int32, (tall, 128), 0) + first
        hits = jnp.concatenate(
            [
                one_hot(links_ref[:1, t : t + 128] == row)
                for t in range(added * nodes, cells * nodes, 128)
            ],
            1,
        )
        both = dot(hits, split[...])
        for u in range(some):
            j = i * some + u
            at = [pl.ds(index_ref[cell, j], 1) for cell in range(added)]
            sums = [
                totals[cell][at[cell], :] + whole[pl.ds(cell * nodes + j, 1), :]
                for cell in range(added)
            ]
            for cell in range(added):
                totals[cell][at[cell], :] = sums[cell]
        summed_ref[pl.ds(first, tall), :] = both[:, :width] + both[:, width:]
        return carry

    lax.fori_loop(0, steps, add, 0)

    def collect(i, carry):
        part = pl.ds(pl.multiple_of(i * 64, 64), 64)
        summed = summed_ref[part, :]
        for total in totals:
            summed = summed + total[part, :]
        summed_ref[part, :] = summed
        return carry

    lax.fori_loop(0, own // 64, collect, 0)


def applied(faces_ref, summed_ref, arrived_ref, mass_ref):
    own, face = summed_ref.shape[0], arrived_ref.shape[0]
    hits = one_hot(lax.broadcasted_iota(jnp.int32, (own, face), 0) == faces_ref[:1, :])
    return mass_ref[...] * (summed_ref[...] + dot(hits, arrived_ref[...]))


def first_body(
    face_ref, faces_ref, summed_ref, arrived_ref, mass_ref, wave_ref,
    current_ref, scaled_ref, sent_ref, picked,
):
    own, width = summed_ref.shape
    image = applied(faces_ref, summed_ref, arrived_ref, mass_ref)
    current_ref[...] = (image - CENTER * wave_ref[...].astype(F32)) / HALF
    scale_rows(own, width, current_ref[...], mass_ref, face_ref, scaled_ref, sent_ref, picked)


def next_body(
    face_ref, faces_ref, summed_ref, arrived_ref, mass_ref, previous_ref,
    current_ref, following_ref, scaled_ref, sent_ref, picked,
):
    own, width = summed_ref.shape
    image = applied(faces_ref, summed_ref, arrived_ref, mass_ref)
    following_ref[...] = 2.0 * (image - CENTER * current_ref[...]) / HALF - previous_ref[
        ...
    ].astype(F32)
    scale_rows(own, width, following_ref[...], mass_ref, face_ref, scaled_ref, sent_ref, picked)


def last_body(
    faces_ref, summed_ref, arrived_ref, mass_ref, previous_ref, current_ref,
    filtered_ref, rounded_ref,
):
    image = applied(faces_ref, summed_ref, arrived_ref, mass_ref)
    filtered = 2.0 * (image - CENTER * current_ref[...]) / HALF - previous_ref[...].astype(F32)
    filtered_ref[...] = filtered
    rounded_ref[...] = filtered.astype(BF16)


def gram_body(core_ref, rows_ref, blocks_ref):
    cores, chips = rows_ref.shape[:2]
    width = rows_ref.shape[3]
    groups = chips * cores
    group = [rows_ref[g % cores, g // cores] for g in range(groups)]
    half = blocks_ref.shape[0]

    def blocks(first):
        at = 0
        for g in range(groups):
            wanted = [h for h in range(g, groups) if first <= at + h - g < first + half]
            if wanted:
                panel = lax.dot_general(
                    group[g], jnp.concatenate([group[h] for h in wanted], 1),
                    (((0,), (0,)), ((), ())), preferred_element_type=F32,
                )
                for i, h in enumerate(wanted):
                    blocks_ref[at + h - g - first] = panel[
                        :, i * width : (i + 1) * width
                    ].astype(BF16)
            at += groups - g

    for core in range(cores):
        pl.when(core_ref[0] == core)(functools.partial(blocks, core * half))


def correct_body(nodes, core_ref, blocks_ref, rows_ref, change_ref, scale_ref, excess, first, second):
    cores, chips, own, width = rows_ref.shape
    groups = chips * cores
    states = groups * width
    same = lax.broadcasted_iota(jnp.int32, (width, width), 0) == lax.broadcasted_iota(
        jnp.int32, (width, width), 1
    )
    places = [(g, h) for g in range(groups) for h in range(g, groups)]
    diagonal = jnp.zeros((width, width), F32)
    for at, (g, h) in enumerate(places):
        if g == h:
            diagonal = diagonal + jnp.where(same, blocks_ref[at].astype(F32), 0.0)
    trace = jnp.sum(jnp.sum(diagonal, axis=0, keepdims=True), axis=1, keepdims=True)
    unit = states / trace
    for at, (g, h) in enumerate(places):
        block = blocks_ref[at].astype(F32) * unit
        if g == h:
            block = block - same.astype(F32)
        block = block.astype(BF16)
        excess[g * width : (g + 1) * width, h * width : (h + 1) * width] = block
        if g != h:
            excess[h * width : (h + 1) * width, g * width : (g + 1) * width] = block.T
    scale = 1.0 / jnp.sqrt(trace / (states * nodes))
    scale_ref[...] = jnp.broadcast_to(scale, scale_ref.shape)

    def at_core(rows):
        starts = [pl.multiple_of((cores * p + core_ref[0]) * width, width) for p in range(chips)]
        return jnp.concatenate([excess[rows, pl.ds(s, width)] for s in starts], 1)

    tall = states // 4
    parts = [slice(i * tall, (i + 1) * tall) for i in range(4)]
    for rows in parts:
        second[rows, :] = at_core(rows)
    for rows in parts:
        square = dot(excess[rows, :], second[...])
        first[rows, :] = (0.0625 * square - 0.3125 * second[rows, :].astype(F32)).astype(BF16)
    for rows in parts:
        cube = dot(excess[rows, :], first[...]) + 0.375 * at_core(rows).astype(F32)
        second[rows, :] = cube.astype(BF16)
    for rows in parts:
        added = dot(excess[rows, :], second[...]) - 0.5 * at_core(rows).astype(F32)
        first[rows, :] = (added * scale).astype(BF16)
    for p in range(own // width):
        some = slice(p * width, (p + 1) * width)
        every = jnp.concatenate([rows_ref[g % cores, g // cores, some, :] for g in range(groups)], 1)
        change = dot(every, first[...]).astype(BF16)
        for q in range(chips):
            change_ref[q, some, :] = change[:, q * width : (q + 1) * width]


def finish_body(filtered_ref, change_ref, scale_ref, rotated_ref):
    rotated_ref[...] = filtered_ref[...] * scale_ref[:1, :] + change_ref[...].astype(F32)


def passed_along(value, steps):
    count = lax.axis_size(DOM)
    initial, last = max(0, -steps), min(count, count - steps)
    return lax.ppermute(value, DOM, [(source, source + steps) for source in range(initial, last)])


def exchanged(pieces, axes):
    return lax.all_to_all(pieces, axes, split_axis=0, concat_axis=0, tiled=True)


def sum_of_share(array, axes):
    peers = lax.axis_size(axes)
    pieces = array.reshape(peers, array.shape[0] // peers, array.shape[1])
    return exchanged(pieces, axes).astype(F32).sum(axis=0).astype(BF16)


def shares_of_all(array, axes):
    peers = lax.axis_size(axes)
    arrived = exchanged(jnp.broadcast_to(array, (peers, *array.shape)), axes)
    return arrived.reshape(peers * array.shape[0], array.shape[1])


def on_device(wavefunctions, mass_scale, cell_matrices, connectivity, face_index):
    own, width = wavefunctions.shape
    face = face_index.shape[0]
    cells, cell_nodes = connectivity.shape
    extent = own + face
    entries = cells * cell_nodes
    domains = lax.axis_size(DOM)
    bands = lax.axis_size(BAND)

    mass = jnp.broadcast_to(mass_scale[:, None], (own, width))
    links = jnp.broadcast_to(connectivity.reshape(1, entries), (8, entries))
    copied = cells // 2
    column = jnp.broadcast_to(
        connectivity[copied:].reshape(-1, 1), ((cells - copied) * cell_nodes, 128)
    )
    faces = jnp.broadcast_to(face_index.reshape(1, face), (8, face))
    face_list = face_index.reshape(1, face)

    picked = pltpu.VMEM((face, width), F32)
    scaled_shape = shape((extent, width), F32)
    rows_shape = shape((face, width), BF16)
    wide = shape((own, width), F32)
    start = call(
        start_body, "scaled_start", [IN_SMEM] + [IN_VMEM] * 2, [scaled_shape, rows_shape], [picked],
        10**6, 3 * 2**20,
    )
    gathering = [pltpu.VMEM((entries, width), F32), pltpu.VMEM((extent, width), BF16)]
    opening = call(
        functools.partial(opening_body, own, face), "opening_products",
        [IN_SMEM] + [IN_VMEM] * 3 + [IN_ANY],
        [
            shape((entries, width), F32), shape((entries, 2 * face), BF16),
            shape((face, 2 * face), BF16), shape((face, width), F32),
        ],
        gathering + [pltpu.VMEM(cell_matrices.shape, BF16), pltpu.SemaphoreType.DMA],
        8 * 10**9, 16 * 2**20, 45,
    )
    local = call(
        functools.partial(local_body, own, face), "local_products", [IN_SMEM] + [IN_VMEM] * 4,
        [shape((entries, width), F32), shape((face, width), F32)], gathering,
        5 * 10**9, 16 * 2**20,
    )
    returned = call(
        returned_body, "returned", [IN_VMEM] * 3, rows_shape, [], 10**8, 2**20,
    )
    assemble = call(
        assemble_body, "assembled", [IN_SMEM] + [IN_VMEM] * 4, wide,
        [
            pltpu.VMEM((copied * cell_nodes, width), F32),
            pltpu.VMEM((entries - copied * cell_nodes, 2 * width), BF16),
        ]
        + [pltpu.VMEM((extent, width), F32)] * copied,
        5 * 10**9, 16 * 2**20,
    )

    scaled, rows = start(face_list, wavefunctions, mass)
    previous, current = None, wavefunctions
    for sweep in range(DEGREE):
        received = passed_along(rows, -1)
        if sweep == 0:
            products, spread, block, sent = opening(
                connectivity, links, column, scaled, cell_matrices
            )
        else:
            products, sent = local(connectivity, links, column, scaled, cell_matrices)
        arrived = passed_along(returned(sent, block, received), 1)
        summed = assemble(connectivity, links, products, spread, received)
        parts = (summed, arrived, mass)
        if sweep == DEGREE - 1:
            filtered, rounded = call(
                last_body, "filtered", [IN_VMEM] * 6, [wide, shape((own, width), BF16)], [],
                10**9, 6 * 2**20,
            )(faces, *parts, previous, current)
        elif sweep == 0:
            following, scaled, rows = call(
                first_body, "first_step", [IN_SMEM] + [IN_VMEM] * 5,
                [wide, scaled_shape, rows_shape], [picked], 10**9, 6 * 2**20,
            )(face_list, faces, *parts, current)
            previous, current = current, following
        else:
            following, scaled, rows = call(
                next_body, "next_step", [IN_SMEM] + [IN_VMEM] * 6,
                [wide, scaled_shape, rows_shape], [picked], 10**9, 6 * 2**20,
            )(face_list, faces, *parts, previous, current)
            previous, current = current, following

    chips, cores = lax.axis_size(CHIP), lax.axis_size(CORE)
    mine = exchanged(rounded.reshape(chips, own // chips, width), CHIP)
    both = exchanged(jnp.broadcast_to(mine, (cores, *mine.shape)), CORE)
    pairs = bands * (bands + 1) // 2
    half = pairs // cores
    core = lax.axis_index(CORE).astype(jnp.int32).reshape(1)
    gram = call(
        gram_body, "gram", [IN_SMEM, IN_VMEM], shape((half, width, width), BF16), [],
        10**9, 3 * 2**20,
    )(core, both)
    gram = sum_of_share(gram.reshape(half * width, width), PLANE)
    columns = lax.axis_size(COLUMN)
    gram = exchanged(jnp.broadcast_to(gram, (columns, *gram.shape)), COLUMN)
    gram = gram.astype(F32).sum(axis=0).astype(BF16)
    for axes in (PLANE, CORE):
        gram = shares_of_all(gram, axes)
    states = bands * width
    change, scale = call(
        functools.partial(correct_body, own * domains), "correction", [IN_SMEM, IN_VMEM, IN_VMEM],
        [shape(mine.shape, BF16), shape((8, width), F32)],
        [
            pltpu.VMEM((states, states), BF16),
            pltpu.VMEM((states, chips * width), BF16),
            pltpu.VMEM((states, chips * width), BF16),
        ],
        4 * 10**9, 8 * 2**20,
    )(core, gram.reshape(pairs, width, width), both)
    change = exchanged(change, CHIP).reshape(own, width)
    return call(finish_body, "rotated", [IN_VMEM] * 3, wide, [], 10**6, 3 * 2**20)(
        filtered, change, scale
    )


def solution(mesh):
    finer = Mesh(
        mesh.devices.reshape(4, 4, 2, 4, 2), ("dom_0", "dom_1", "dom_2", "band_0", "band_1")
    )
    placed = (P(DOM, BAND), P(DOM), P(DOM, None, None), P(DOM, None), P(DOM))
    return jax.shard_map(
        on_device, mesh=finer, in_specs=placed, out_specs=P(DOM, BAND), check_vma=False
    )
```

```python
import functools

import jax
import jax.numpy as jnp
from jax import lax
from jax.experimental import pallas as pl
from jax.experimental.pallas import tpu as pltpu
from jax.sharding import Mesh
from jax.sharding import PartitionSpec as P

STATES = 1024
DEGREE = 3
CENTER = 5.0
HALF = 5.0
DOM = ("dom_0", "dom_1", "dom_2")
BAND = ("band_0", "band_1")
PLANE = ("dom_0", "dom_1")
COLUMN = ("dom_2", "band_0")
CHIP = ("band_0",)
CORE = ("band_1",)
F32 = jnp.float32
BF16 = jnp.bfloat16
IN_VMEM = pl.BlockSpec(memory_space=pltpu.VMEM)
IN_SMEM = pl.BlockSpec(memory_space=pltpu.SMEM)
IN_ANY = pl.BlockSpec(memory_space=pl.ANY)


def shape(dims, dtype):
    return jax.ShapeDtypeStruct(dims, dtype)


def call(body, name, ins, outs, scratch=(), flops=0, moved=0, vmem=32):
    return pl.pallas_call(
        body,
        in_specs=ins,
        out_specs=jax.tree.map(lambda _: IN_VMEM, outs),
        out_shape=outs,
        scratch_shapes=list(scratch),
        compiler_params=pltpu.CompilerParams(vmem_limit_bytes=vmem * 2**20),
        cost_estimate=pl.CostEstimate(flops=flops, bytes_accessed=moved, transcendentals=0),
        name=name,
    )


def dot(a, b):
    return jnp.dot(a, b, preferred_element_type=F32)


def halves(a, axis=1):
    high = a.astype(BF16)
    return jnp.concatenate([high, (a - high.astype(F32)).astype(BF16)], axis)


def one_hot(hit):
    return jnp.where(hit, 1.0, 0.0).astype(BF16)


def scale_rows(own, width, values, mass_ref, face_ref, scaled_ref, rows_ref, picked):
    scaled_ref[:own, :] = (mass_ref[...] * values).astype(BF16).astype(F32)
    scaled_ref[own:, :] = jnp.zeros((scaled_ref.shape[0] - own, width), F32)

    def take(i, carry):
        rows = [scaled_ref[pl.ds(face_ref[0, i * 8 + u], 1), :] for u in range(8)]
        picked[pl.ds(pl.multiple_of(i * 8, 8), 8), :] = jnp.concatenate(rows, 0)
        return carry

    lax.fori_loop(0, picked.shape[0] // 8, take, 0)
    rows_ref[...] = picked[...].astype(BF16)


def start_body(face_ref, wave_ref, mass_ref, scaled_ref, rows_ref, picked):
    own, width = wave_ref.shape
    scale_rows(
        own, width, wave_ref[...].astype(F32), mass_ref, face_ref, scaled_ref, rows_ref, picked
    )


def face_hits(links_ref, own, face, cell, nodes):
    links = links_ref[:1, cell * nodes : (cell + 1) * nodes]
    return one_hot(links == lax.broadcasted_iota(jnp.int32, (face, nodes), 0) + own)


def local_products(
    own, face, index_ref, links_ref, column_ref, scaled_ref, cells_ref, products_ref, sent_ref,
    held, narrow, received=None,
):
    cells, nodes = index_ref.shape
    extent, width = scaled_ref.shape
    named_from = cells - column_ref.shape[0] // nodes
    copied = named_from if received is None else cells - 1
    narrow[...] = scaled_ref[...].astype(BF16)
    sent_ref[...] = jnp.zeros_like(sent_ref)

    def part(cell):
        return slice(cell * nodes, (cell + 1) * nodes)

    def by_one_hot(cell):
        named = column_ref[part(cell - named_from), :]
        lane = lax.broadcasted_iota(jnp.int32, (nodes, 128), 1)
        hits = jnp.concatenate([one_hot(named == lane + t) for t in range(0, extent, 128)], 1)
        held[part(cell), :] = dot(hits, narrow[...])

    def multiply(cell):
        product = dot(cells_ref[cell], held[part(cell), :].astype(BF16))
        products_ref[part(cell), :] = product
        both = dot(face_hits(links_ref, own, face, cell, nodes), halves(product))
        sent_ref[...] += both[:, :width] + both[:, width:]

    def copy_rows(cell):
        for at in range(0, nodes, 8):
            rows = [scaled_ref[pl.ds(index_ref[cell, at + u], 1), :] for u in range(8)]
            held[cell * nodes + at : cell * nodes + at + 8, :] = jnp.concatenate(rows, 0)

    beside = [[] for _ in range(copied)]
    for i, cell in enumerate(range(copied, cells)):
        beside[i].append(functools.partial(by_one_hot, cell))
    after = []
    if received is None:
        waiting = list(range(copied, cells)) + list(range(copied))
        done = 0
        for stage in range(cells - copied, copied):
            for cell in waiting[done : done + 3]:
                if cell >= copied or cell < stage:
                    beside[stage].append(functools.partial(multiply, cell))
                    done += 1
    else:
        for cell in range(cells):
            stage = min(1 + cell // 2 if cell < 4 else cell - 1, copied - 1)
            beside[stage].append(functools.partial(received, cell))
        waiting = list(range(cells))
        done = 0
        for stage in range(3, copied):
            beside[stage].append(functools.partial(multiply, waiting[done]))
            done += 1
    after = [functools.partial(multiply, cell) for cell in waiting[done:]]
    for cell in range(copied):
        for task in beside[cell]:
            task()
        copy_rows(cell)
    for task in after:
        task()


def opening_body(
    own, face, index_ref, links_ref, column_ref, scaled_ref, matrices_ref, products_ref,
    spread_ref, block_ref, sent_ref, low_ref, held, narrow, cells_ref, block, sems,
):
    cells, nodes = index_ref.shape
    copies = [
        pltpu.make_async_copy(matrices_ref.at[c], cells_ref.at[c], sems.at[c])
        for c in range(cells)
    ]
    for copy in copies:
        copy.start()
    block[...] = jnp.zeros_like(block)

    def received(cell):
        copies[cell].wait()
        hits = face_hits(links_ref, own, face, cell, nodes)
        columns = lax.dot_general(
            cells_ref[cell], hits, (((1,), (1,)), ((), ())), preferred_element_type=F32
        )
        both = halves(columns)
        spread_ref[cell * nodes : (cell + 1) * nodes, :] = both
        block[...] += dot(hits, both)
        low = jnp.max(jnp.abs(both[:, face:].astype(F32)), axis=0, keepdims=True)
        low_ref[cell : cell + 1, :] = jnp.max(low, axis=1, keepdims=True) + jnp.zeros(
            (1, low_ref.shape[1]), F32
        )

    local_products(
        own, face, index_ref, links_ref, column_ref, scaled_ref, cells_ref, products_ref, sent_ref,
        held, narrow, received,
    )
    total = block[...]
    block_ref[...] = halves(total[:, :face] + total[:, face:])


def local_body(
    own, face, index_ref, links_ref, column_ref, scaled_ref, cells_ref, products_ref, sent_ref,
    held, narrow,
):
    local_products(
        own, face, index_ref, links_ref, column_ref, scaled_ref, cells_ref, products_ref, sent_ref,
        held, narrow,
    )


def returned_body(sent_ref, block_ref, rows_ref, total_ref):
    rows = rows_ref[...]
    total_ref[...] = sent_ref[...] + dot(block_ref[...], jnp.concatenate([rows, rows], 0))


def assemble_body(
    index_ref, low_ref, links_ref, products_ref, spread_ref, rows_ref, summed_ref, whole, split,
    *totals
):
    cells, nodes = index_ref.shape
    own, width = summed_ref.shape
    added = len(totals)
    rows = rows_ref[...]
    face = rows.shape[0]
    for cell in range(cells):
        part = slice(cell * nodes, (cell + 1) * nodes)
        whole[part, :] = products_ref[part, :] + dot(spread_ref[part, :face], rows)

        def add_low(part=part):
            whole[part, :] += dot(spread_ref[part, face:], rows_ref[...])

        pl.when(low_ref[cell, 0] != 0.0)(add_low)
    split[...] = halves(whole[added * nodes :, :])
    for total in totals:
        total[...] = jnp.zeros_like(total)
    steps = 4
    some = nodes // steps
    tall = own // steps

    def add(i, carry):
        first = pl.multiple_of(i * tall, tall)
        row = lax.broadcasted_iota(jnp.int32, (tall, 128), 0) + first
        hits = jnp.concatenate(
            [
                one_hot(links_ref[:1, t : t + 128] == row)
                for t in range(added * nodes, cells * nodes, 128)
            ],
            1,
        )
        both = dot(hits, split[...])
        for u in range(some):
            j = i * some + u
            at = [pl.ds(index_ref[cell, j], 1) for cell in range(added)]
            sums = [
                totals[cell][at[cell], :] + whole[pl.ds(cell * nodes + j, 1), :]
                for cell in range(added)
            ]
            for cell in range(added):
                totals[cell][at[cell], :] = sums[cell]
        summed_ref[pl.ds(first, tall), :] = both[:, :width] + both[:, width:]
        return carry

    lax.fori_loop(0, steps, add, 0)

    def collect(i, carry):
        part = pl.ds(pl.multiple_of(i * 64, 64), 64)
        summed = summed_ref[part, :]
        for total in totals:
            summed = summed + total[part, :]
        summed_ref[part, :] = summed
        return carry

    lax.fori_loop(0, own // 64, collect, 0)


def applied(faces_ref, summed_ref, arrived_ref, mass_ref):
    own, width = summed_ref.shape
    face = arrived_ref.shape[0]
    hits = one_hot(lax.broadcasted_iota(jnp.int32, (own, face), 0) == faces_ref[:1, :])
    added = dot(hits, halves(arrived_ref[...]))
    return mass_ref[...] * (summed_ref[...] + (added[:, :width] + added[:, width:]))


def first_body(
    face_ref, faces_ref, summed_ref, arrived_ref, mass_ref, wave_ref,
    current_ref, scaled_ref, sent_ref, picked,
):
    own, width = summed_ref.shape
    image = applied(faces_ref, summed_ref, arrived_ref, mass_ref)
    current_ref[...] = (image - CENTER * wave_ref[...].astype(F32)) / HALF
    scale_rows(own, width, current_ref[...], mass_ref, face_ref, scaled_ref, sent_ref, picked)


def next_body(
    face_ref, faces_ref, summed_ref, arrived_ref, mass_ref, previous_ref,
    current_ref, following_ref, scaled_ref, sent_ref, picked,
):
    own, width = summed_ref.shape
    image = applied(faces_ref, summed_ref, arrived_ref, mass_ref)
    following_ref[...] = 2.0 * (image - CENTER * current_ref[...]) / HALF - previous_ref[
        ...
    ].astype(F32)
    scale_rows(own, width, following_ref[...], mass_ref, face_ref, scaled_ref, sent_ref, picked)


def last_body(
    faces_ref, summed_ref, arrived_ref, mass_ref, previous_ref, current_ref,
    filtered_ref, rounded_ref,
):
    image = applied(faces_ref, summed_ref, arrived_ref, mass_ref)
    filtered = 2.0 * (image - CENTER * current_ref[...]) / HALF - previous_ref[...].astype(F32)
    filtered_ref[...] = filtered
    rounded_ref[...] = filtered.astype(BF16)


def gram_body(core_ref, rows_ref, blocks_ref):
    cores, chips = rows_ref.shape[:2]
    width = rows_ref.shape[3]
    groups = chips * cores
    group = [rows_ref[g % cores, g // cores] for g in range(groups)]
    half = blocks_ref.shape[0]

    def blocks(first):
        at = 0
        for g in range(groups):
            wanted = [h for h in range(g, groups) if first <= at + h - g < first + half]
            if wanted:
                panel = lax.dot_general(
                    group[g], jnp.concatenate([group[h] for h in wanted], 1),
                    (((0,), (0,)), ((), ())), preferred_element_type=F32,
                )
                for i, h in enumerate(wanted):
                    blocks_ref[at + h - g - first] = panel[
                        :, i * width : (i + 1) * width
                    ].astype(BF16)
            at += groups - g

    for core in range(cores):
        pl.when(core_ref[0] == core)(functools.partial(blocks, core * half))


def correct_body(nodes, core_ref, blocks_ref, rows_ref, change_ref, scale_ref, excess, first, second):
    cores, chips, own, width = rows_ref.shape
    groups = chips * cores
    states = groups * width
    same = lax.broadcasted_iota(jnp.int32, (width, width), 0) == lax.broadcasted_iota(
        jnp.int32, (width, width), 1
    )
    places = [(g, h) for g in range(groups) for h in range(g, groups)]
    diagonal = jnp.zeros((width, width), F32)
    for at, (g, h) in enumerate(places):
        if g == h:
            diagonal = diagonal + jnp.where(same, blocks_ref[at].astype(F32), 0.0)
    trace = jnp.sum(jnp.sum(diagonal, axis=0, keepdims=True), axis=1, keepdims=True)
    unit = states / trace
    for at, (g, h) in enumerate(places):
        block = blocks_ref[at].astype(F32) * unit
        if g == h:
            block = block - same.astype(F32)
        block = block.astype(BF16)
        excess[g * width : (g + 1) * width, h * width : (h + 1) * width] = block
        if g != h:
            excess[h * width : (h + 1) * width, g * width : (g + 1) * width] = block.T
    scale = 1.0 / jnp.sqrt(trace / (states * nodes))
    scale_ref[...] = jnp.broadcast_to(scale, scale_ref.shape)

    def at_core(rows):
        starts = [pl.multiple_of((cores * p + core_ref[0]) * width, width) for p in range(chips)]
        return jnp.concatenate([excess[rows, pl.ds(s, width)] for s in starts], 1)

    tall = states // 4
    parts = [slice(i * tall, (i + 1) * tall) for i in range(4)]
    for rows in parts:
        second[rows, :] = at_core(rows)
    for rows in parts:
        square = dot(excess[rows, :], second[...])
        first[rows, :] = (0.0625 * square - 0.3125 * second[rows, :].astype(F32)).astype(BF16)
    for rows in parts:
        cube = dot(excess[rows, :], first[...]) + 0.375 * at_core(rows).astype(F32)
        second[rows, :] = cube.astype(BF16)
    for rows in parts:
        added = dot(excess[rows, :], second[...]) - 0.5 * at_core(rows).astype(F32)
        first[rows, :] = (added * scale).astype(BF16)
    for p in range(own // width):
        some = slice(p * width, (p + 1) * width)
        every = jnp.concatenate([rows_ref[g % cores, g // cores, some, :] for g in range(groups)], 1)
        change = dot(every, first[...]).astype(BF16)
        for q in range(chips):
            change_ref[q, some, :] = change[:, q * width : (q + 1) * width]


def finish_body(filtered_ref, change_ref, scale_ref, rotated_ref):
    rotated_ref[...] = filtered_ref[...] * scale_ref[:1, :] + change_ref[...].astype(F32)


def passed_along(value, steps):
    count = lax.axis_size(DOM)
    initial, last = max(0, -steps), min(count, count - steps)
    return lax.ppermute(value, DOM, [(source, source + steps) for source in range(initial, last)])


def exchanged(pieces, axes):
    return lax.all_to_all(pieces, axes, split_axis=0, concat_axis=0, tiled=True)


def sum_of_share(array, axes):
    peers = lax.axis_size(axes)
    pieces = array.reshape(peers, array.shape[0] // peers, array.shape[1])
    return exchanged(pieces, axes).astype(F32).sum(axis=0).astype(BF16)


def shares_of_all(array, axes):
    peers = lax.axis_size(axes)
    arrived = exchanged(jnp.broadcast_to(array, (peers, *array.shape)), axes)
    return arrived.reshape(peers * array.shape[0], array.shape[1])


def on_device(wavefunctions, mass_scale, cell_matrices, connectivity, face_index):
    own, width = wavefunctions.shape
    face = face_index.shape[0]
    cells, cell_nodes = connectivity.shape
    extent = own + face
    entries = cells * cell_nodes
    domains = lax.axis_size(DOM)
    bands = lax.axis_size(BAND)

    mass = jnp.broadcast_to(mass_scale[:, None], (own, width))
    links = jnp.broadcast_to(connectivity.reshape(1, entries), (8, entries))
    copied = cells // 2
    column = jnp.broadcast_to(
        connectivity[copied + 1 :].reshape(-1, 1), ((cells - copied - 1) * cell_nodes, 128)
    )
    faces = jnp.broadcast_to(face_index.reshape(1, face), (8, face))
    face_list = face_index.reshape(1, face)

    picked = pltpu.VMEM((face, width), F32)
    scaled_shape = shape((extent, width), F32)
    rows_shape = shape((face, width), BF16)
    wide = shape((own, width), F32)
    start = call(
        start_body, "scaled_start", [IN_SMEM] + [IN_VMEM] * 2, [scaled_shape, rows_shape], [picked],
        10**6, 3 * 2**20,
    )
    gathering = [pltpu.VMEM((entries, width), F32), pltpu.VMEM((extent, width), BF16)]
    opening = call(
        functools.partial(opening_body, own, face), "opening_products",
        [IN_SMEM] + [IN_VMEM] * 3 + [IN_ANY],
        [
            shape((entries, width), F32), shape((entries, 2 * face), BF16),
            shape((face, 2 * face), BF16), shape((face, width), F32), shape((cells, 128), F32),
        ],
        gathering
        + [
            pltpu.VMEM(cell_matrices.shape, BF16), pltpu.VMEM((face, 2 * face), F32),
            pltpu.SemaphoreType.DMA((cells,)),
        ],
        8 * 10**9, 16 * 2**20, 45,
    )
    local = call(
        functools.partial(local_body, own, face), "local_products", [IN_SMEM] + [IN_VMEM] * 4,
        [shape((entries, width), F32), shape((face, width), F32)], gathering,
        5 * 10**9, 16 * 2**20,
    )
    returned = call(
        returned_body, "returned", [IN_VMEM] * 3, shape((face, width), F32), [], 10**8, 2**20,
    )
    assemble = call(
        assemble_body, "assembled", [IN_SMEM] * 2 + [IN_VMEM] * 4, wide,
        [
            pltpu.VMEM((entries, width), F32),
            pltpu.VMEM((entries - copied * cell_nodes, 2 * width), BF16),
        ]
        + [pltpu.VMEM((extent, width), F32)] * copied,
        5 * 10**9, 16 * 2**20,
    )

    scaled, rows = start(face_list, wavefunctions, mass)
    previous, current = None, wavefunctions
    for sweep in range(DEGREE):
        received = passed_along(rows, -1)
        if sweep == 0:
            products, spread, block, sent, low = opening(
                connectivity, links, column, scaled, cell_matrices
            )
        else:
            products, sent = local(connectivity, links, column, scaled, cell_matrices)
        arrived = passed_along(returned(sent, block, received), 1)
        summed = assemble(connectivity, low, links, products, spread, received)
        parts = (summed, arrived, mass)
        if sweep == DEGREE - 1:
            filtered, rounded = call(
                last_body, "filtered", [IN_VMEM] * 6, [wide, shape((own, width), BF16)], [],
                10**9, 6 * 2**20,
            )(faces, *parts, previous, current)
        elif sweep == 0:
            following, scaled, rows = call(
                first_body, "first_step", [IN_SMEM] + [IN_VMEM] * 5,
                [wide, scaled_shape, rows_shape], [picked], 10**9, 6 * 2**20,
            )(face_list, faces, *parts, current)
            previous, current = current, following
        else:
            following, scaled, rows = call(
                next_body, "next_step", [IN_SMEM] + [IN_VMEM] * 6,
                [wide, scaled_shape, rows_shape], [picked], 10**9, 6 * 2**20,
            )(face_list, faces, *parts, previous, current)
            previous, current = current, following

    chips, cores = lax.axis_size(CHIP), lax.axis_size(CORE)
    mine = exchanged(rounded.reshape(chips, own // chips, width), CHIP)
    both = exchanged(jnp.broadcast_to(mine, (cores, *mine.shape)), CORE)
    pairs = bands * (bands + 1) // 2
    half = pairs // cores
    core = lax.axis_index(CORE).astype(jnp.int32).reshape(1)
    gram = call(
        gram_body, "gram", [IN_SMEM, IN_VMEM], shape((half, width, width), BF16), [],
        10**9, 3 * 2**20,
    )(core, both)
    gram = sum_of_share(gram.reshape(half * width, width), PLANE)
    columns = lax.axis_size(COLUMN)
    gram = exchanged(jnp.broadcast_to(gram, (columns, *gram.shape)), COLUMN)
    gram = gram.astype(F32).sum(axis=0).astype(BF16)
    for axes in (PLANE, CORE):
        gram = shares_of_all(gram, axes)
    states = bands * width
    change, scale = call(
        functools.partial(correct_body, own * domains), "correction", [IN_SMEM, IN_VMEM, IN_VMEM],
        [shape(mine.shape, BF16), shape((8, width), F32)],
        [
            pltpu.VMEM((states, states), BF16),
            pltpu.VMEM((states, chips * width), BF16),
            pltpu.VMEM((states, chips * width), BF16),
        ],
        4 * 10**9, 8 * 2**20,
    )(core, gram.reshape(pairs, width, width), both)
    change = exchanged(change, CHIP).reshape(own, width)
    return call(finish_body, "rotated", [IN_VMEM] * 3, wide, [], 10**6, 3 * 2**20)(
        filtered, change, scale
    )


def solution(mesh):
    finer = Mesh(
        mesh.devices.reshape(4, 4, 2, 4, 2), ("dom_0", "dom_1", "dom_2", "band_0", "band_1")
    )
    placed = (P(DOM, BAND), P(DOM), P(DOM, None, None), P(DOM, None), P(DOM))
    return jax.shard_map(
        on_device, mesh=finer, in_specs=placed, out_specs=P(DOM, BAND), check_vma=False
    )
```

```python
import functools

import jax
import jax.numpy as jnp
from jax import lax
from jax.experimental import pallas as pl
from jax.experimental.pallas import tpu as pltpu
from jax.sharding import Mesh
from jax.sharding import PartitionSpec as P

STATES = 1024
DEGREE = 3
CENTER = 5.0
HALF = 5.0
DOM = ("dom_0", "dom_1", "dom_2")
BAND = ("band_0", "band_1")
PLANE = ("dom_0", "dom_1")
COLUMN = ("dom_2", "band_0")
CHIP = ("band_0",)
CORE = ("band_1",)
F32 = jnp.float32
BF16 = jnp.bfloat16
IN_VMEM = pl.BlockSpec(memory_space=pltpu.VMEM)
IN_SMEM = pl.BlockSpec(memory_space=pltpu.SMEM)
IN_ANY = pl.BlockSpec(memory_space=pl.ANY)


def shape(dims, dtype):
    return jax.ShapeDtypeStruct(dims, dtype)


def call(body, name, ins, outs, scratch=(), flops=0, moved=0, vmem=32):
    return pl.pallas_call(
        body,
        in_specs=ins,
        out_specs=jax.tree.map(lambda _: IN_VMEM, outs),
        out_shape=outs,
        scratch_shapes=list(scratch),
        compiler_params=pltpu.CompilerParams(vmem_limit_bytes=vmem * 2**20),
        cost_estimate=pl.CostEstimate(flops=flops, bytes_accessed=moved, transcendentals=0),
        name=name,
    )


def dot(a, b):
    return jnp.dot(a, b, preferred_element_type=F32)


def halves(a, axis=1):
    high = a.astype(BF16)
    return jnp.concatenate([high, (a - high.astype(F32)).astype(BF16)], axis)


def one_hot(hit):
    return jnp.where(hit, 1.0, 0.0).astype(BF16)


def pick_rows(face_ref, scaled_ref, rows_ref, picked):
    def take(i, carry):
        rows = [scaled_ref[pl.ds(face_ref[0, i * 8 + u], 1), :] for u in range(8)]
        picked[pl.ds(pl.multiple_of(i * 8, 8), 8), :] = jnp.concatenate(rows, 0)
        return carry

    lax.fori_loop(0, picked.shape[0] // 8, take, 0)
    rows_ref[...] = picked[...].astype(BF16)


def scale_rows(own, width, values, mass_ref, face_ref, scaled_ref, rows_ref, picked):
    scaled_ref[:own, :] = (mass_ref[...] * values).astype(BF16).astype(F32)
    scaled_ref[own:, :] = jnp.zeros((scaled_ref.shape[0] - own, width), F32)
    pick_rows(face_ref, scaled_ref, rows_ref, picked)


def face_hits(links_ref, own, face, cell, nodes):
    links = links_ref[:1, cell * nodes : (cell + 1) * nodes]
    return one_hot(links == lax.broadcasted_iota(jnp.int32, (face, nodes), 0) + own)


def take_entries(index_ref, column_ref, scaled_ref, held, narrow):
    cells, nodes = index_ref.shape
    extent, width = scaled_ref.shape
    copied = cells - column_ref.shape[0] // nodes
    narrow[...] = scaled_ref[...].astype(BF16)
    steps = 4
    some = nodes // steps
    rest = column_ref.shape[0] // steps

    def take(i, carry):
        first = pl.multiple_of(i * rest, rest)
        named = column_ref[pl.ds(first, rest), :]
        lane = lax.broadcasted_iota(jnp.int32, (rest, 128), 1)
        hits = jnp.concatenate([one_hot(named == lane + t) for t in range(0, extent, 128)], 1)
        product = dot(hits, narrow[...])
        for k in range(some // 8):
            for cell in range(copied):
                at = i * some + k * 8
                rows = [scaled_ref[pl.ds(index_ref[cell, at + u], 1), :] for u in range(8)]
                held[pl.ds(pl.multiple_of(cell * nodes + at, 8), 8), :] = jnp.concatenate(rows, 0)
        held[pl.ds(copied * nodes + first, rest), :] = product
        return carry

    lax.fori_loop(0, steps, take, 0)


def opening_body(
    own, face, index_ref, links_ref, column_ref, scaled_ref, matrices_ref, products_ref,
    spread_ref, block_ref, sent_ref, held, narrow, cells_ref, sem,
):
    copy = pltpu.make_async_copy(matrices_ref, cells_ref, sem)
    copy.start()
    take_entries(index_ref, column_ref, scaled_ref, held, narrow)
    copy.wait()
    cells, nodes = index_ref.shape
    width = scaled_ref.shape[1]
    total = jnp.zeros((face, 2 * width), F32)
    block = jnp.zeros((face, 2 * face), F32)
    for cell in range(cells):
        part = slice(cell * nodes, (cell + 1) * nodes)
        hits = face_hits(links_ref, own, face, cell, nodes)
        columns = lax.dot_general(
            cells_ref[cell], hits, (((1,), (1,)), ((), ())), preferred_element_type=F32
        )
        both = halves(columns)
        spread_ref[part, :] = both
        block = block + dot(hits, both)
        product = dot(cells_ref[cell], held[part, :].astype(BF16))
        products_ref[part, :] = product
        total = total + dot(hits, halves(product))
    sent_ref[...] = total[:, :width] + total[:, width:]
    block_ref[...] = halves(block[:, :face] + block[:, face:])


def local_body(
    own, face, index_ref, links_ref, column_ref, scaled_ref, cells_ref, products_ref, sent_ref,
    held, narrow,
):
    take_entries(index_ref, column_ref, scaled_ref, held, narrow)
    cells, nodes = index_ref.shape
    width = scaled_ref.shape[1]
    total = jnp.zeros((face, 2 * width), F32)
    for cell in range(cells):
        part = slice(cell * nodes, (cell + 1) * nodes)
        product = dot(cells_ref[cell], held[part, :].astype(BF16))
        products_ref[part, :] = product
        total = total + dot(face_hits(links_ref, own, face, cell, nodes), halves(product))
    sent_ref[...] = total[:, :width] + total[:, width:]


def returned_body(sent_ref, block_ref, rows_ref, total_ref):
    rows = rows_ref[...]
    total_ref[...] = sent_ref[...] + dot(block_ref[...], jnp.concatenate([rows, rows], 0))


def assemble_body(
    index_ref, links_ref, products_ref, spread_ref, rows_ref, summed_ref, whole, split, *totals
):
    cells, nodes = index_ref.shape
    own, width = summed_ref.shape
    added = len(totals)
    rows = rows_ref[...]
    twice = jnp.concatenate([rows, rows], 0)
    for cell in range(cells):
        part = slice(cell * nodes, (cell + 1) * nodes)
        product = products_ref[part, :] + dot(spread_ref[part, :], twice)
        if cell < added:
            whole[part, :] = product
        else:
            split[(cell - added) * nodes : (cell - added + 1) * nodes, :] = halves(product)
    for total in totals:
        total[...] = jnp.zeros_like(total)
    steps = 4
    some = nodes // steps
    tall = own // steps

    def add(i, carry):
        first = pl.multiple_of(i * tall, tall)
        row = lax.broadcasted_iota(jnp.int32, (tall, 128), 0) + first
        hits = jnp.concatenate(
            [
                one_hot(links_ref[:1, t : t + 128] == row)
                for t in range(added * nodes, cells * nodes, 128)
            ],
            1,
        )
        both = dot(hits, split[...])
        for u in range(some):
            j = i * some + u
            at = [pl.ds(index_ref[cell, j], 1) for cell in range(added)]
            sums = [
                totals[cell][at[cell], :] + whole[pl.ds(cell * nodes + j, 1), :]
                for cell in range(added)
            ]
            for cell in range(added):
                totals[cell][at[cell], :] = sums[cell]
        summed_ref[pl.ds(first, tall), :] = both[:, :width] + both[:, width:]
        return carry

    lax.fori_loop(0, steps, add, 0)

    def collect(i, carry):
        part = pl.ds(pl.multiple_of(i * 64, 64), 64)
        summed = summed_ref[part, :]
        for total in totals:
            summed = summed + total[part, :]
        summed_ref[part, :] = summed
        return carry

    lax.fori_loop(0, own // 64, collect, 0)


def applied(faces_ref, summed_ref, arrived_ref, mass_ref):
    own, width = summed_ref.shape
    face = arrived_ref.shape[0]
    hits = one_hot(lax.broadcasted_iota(jnp.int32, (own, face), 0) == faces_ref[:1, :])
    added = dot(hits, halves(arrived_ref[...]))
    return mass_ref[...] * (summed_ref[...] + (added[:, :width] + added[:, width:]))


def first_body(
    face_ref, faces_ref, summed_ref, arrived_ref, mass_ref, wave_ref,
    current_ref, scaled_ref, sent_ref, picked,
):
    own, width = summed_ref.shape
    image = applied(faces_ref, summed_ref, arrived_ref, mass_ref)
    current_ref[...] = (image - CENTER * wave_ref[...].astype(F32)) / HALF
    scale_rows(own, width, current_ref[...], mass_ref, face_ref, scaled_ref, sent_ref, picked)


def next_body(
    face_ref, faces_ref, summed_ref, arrived_ref, mass_ref, previous_ref,
    current_ref, following_ref, scaled_ref, sent_ref, picked,
):
    own, width = summed_ref.shape
    image = applied(faces_ref, summed_ref, arrived_ref, mass_ref)
    following_ref[...] = 2.0 * (image - CENTER * current_ref[...]) / HALF - previous_ref[
        ...
    ].astype(F32)
    scale_rows(own, width, following_ref[...], mass_ref, face_ref, scaled_ref, sent_ref, picked)


def last_body(
    faces_ref, summed_ref, arrived_ref, mass_ref, previous_ref, current_ref,
    filtered_ref, rounded_ref,
):
    image = applied(faces_ref, summed_ref, arrived_ref, mass_ref)
    filtered = 2.0 * (image - CENTER * current_ref[...]) / HALF - previous_ref[...].astype(F32)
    filtered_ref[...] = filtered
    rounded_ref[...] = filtered.astype(BF16)


def gram_body(core_ref, rows_ref, blocks_ref):
    cores, chips = rows_ref.shape[:2]
    width = rows_ref.shape[3]
    groups = chips * cores
    group = [rows_ref[g % cores, g // cores] for g in range(groups)]
    half = blocks_ref.shape[0]

    def blocks(first):
        at = 0
        for g in range(groups):
            wanted = [h for h in range(g, groups) if first <= at + h - g < first + half]
            if wanted:
                panel = lax.dot_general(
                    group[g], jnp.concatenate([group[h] for h in wanted], 1),
                    (((0,), (0,)), ((), ())), preferred_element_type=F32,
                )
                for i, h in enumerate(wanted):
                    blocks_ref[at + h - g - first] = panel[
                        :, i * width : (i + 1) * width
                    ].astype(BF16)
            at += groups - g

    for core in range(cores):
        pl.when(core_ref[0] == core)(functools.partial(blocks, core * half))


def correct_body(nodes, core_ref, blocks_ref, rows_ref, change_ref, scale_ref, excess, first, second):
    cores, chips, own, width = rows_ref.shape
    groups = chips * cores
    states = groups * width
    same = lax.broadcasted_iota(jnp.int32, (width, width), 0) == lax.broadcasted_iota(
        jnp.int32, (width, width), 1
    )
    places = [(g, h) for g in range(groups) for h in range(g, groups)]
    diagonal = jnp.zeros((width, width), F32)
    for at, (g, h) in enumerate(places):
        if g == h:
            diagonal = diagonal + jnp.where(same, blocks_ref[at].astype(F32), 0.0)
    trace = jnp.sum(jnp.sum(diagonal, axis=0, keepdims=True), axis=1, keepdims=True)
    unit = states / trace
    for at, (g, h) in enumerate(places):
        block = blocks_ref[at].astype(F32) * unit
        if g == h:
            block = block - same.astype(F32)
        block = block.astype(BF16)
        excess[g * width : (g + 1) * width, h * width : (h + 1) * width] = block
        if g != h:
            excess[h * width : (h + 1) * width, g * width : (g + 1) * width] = block.T
    scale = 1.0 / jnp.sqrt(trace / (states * nodes))
    scale_ref[...] = jnp.broadcast_to(scale, scale_ref.shape)

    def at_core(rows):
        starts = [pl.multiple_of((cores * p + core_ref[0]) * width, width) for p in range(chips)]
        return jnp.concatenate([excess[rows, pl.ds(s, width)] for s in starts], 1)

    tall = states // 4
    parts = [slice(i * tall, (i + 1) * tall) for i in range(4)]
    for rows in parts:
        second[rows, :] = at_core(rows)
    for rows in parts:
        square = dot(excess[rows, :], second[...])
        first[rows, :] = (0.0625 * square - 0.3125 * second[rows, :].astype(F32)).astype(BF16)
    for rows in parts:
        cube = dot(excess[rows, :], first[...]) + 0.375 * at_core(rows).astype(F32)
        second[rows, :] = cube.astype(BF16)
    for rows in parts:
        added = dot(excess[rows, :], second[...]) - 0.5 * at_core(rows).astype(F32)
        first[rows, :] = (added * scale).astype(BF16)
    for p in range(own // width):
        some = slice(p * width, (p + 1) * width)
        every = jnp.concatenate([rows_ref[g % cores, g // cores, some, :] for g in range(groups)], 1)
        change = dot(every, first[...]).astype(BF16)
        for q in range(chips):
            change_ref[q, some, :] = change[:, q * width : (q + 1) * width]


def finish_body(filtered_ref, change_ref, scale_ref, rotated_ref):
    rotated_ref[...] = filtered_ref[...] * scale_ref[:1, :] + change_ref[...].astype(F32)


def passed_along(value, steps):
    count = lax.axis_size(DOM)
    initial, last = max(0, -steps), min(count, count - steps)
    return lax.ppermute(value, DOM, [(source, source + steps) for source in range(initial, last)])


def exchanged(pieces, axes):
    return lax.all_to_all(pieces, axes, split_axis=0, concat_axis=0, tiled=True)


def sum_of_share(array, axes):
    peers = lax.axis_size(axes)
    pieces = array.reshape(peers, array.shape[0] // peers, array.shape[1])
    return exchanged(pieces, axes).astype(F32).sum(axis=0).astype(BF16)


def shares_of_all(array, axes):
    peers = lax.axis_size(axes)
    arrived = exchanged(jnp.broadcast_to(array, (peers, *array.shape)), axes)
    return arrived.reshape(peers * array.shape[0], array.shape[1])


def on_device(wavefunctions, mass_scale, cell_matrices, connectivity, face_index):
    own, width = wavefunctions.shape
    face = face_index.shape[0]
    cells, cell_nodes = connectivity.shape
    extent = own + face
    entries = cells * cell_nodes
    domains = lax.axis_size(DOM)
    bands = lax.axis_size(BAND)

    mass = jnp.broadcast_to(mass_scale[:, None], (own, width))
    links = jnp.broadcast_to(connectivity.reshape(1, entries), (8, entries))
    copied = cells // 2
    column = jnp.broadcast_to(
        connectivity[copied:].reshape(-1, 1), ((cells - copied) * cell_nodes, 128)
    )
    faces = jnp.broadcast_to(face_index.reshape(1, face), (8, face))
    face_list = face_index.reshape(1, face)

    picked = pltpu.VMEM((face, width), F32)
    scaled_shape = shape((extent, width), F32)
    rows_shape = shape((face, width), BF16)
    wide = shape((own, width), F32)
    start = call(
        pick_rows, "face_rows", [IN_SMEM, IN_VMEM], rows_shape, [picked], 10**6, 2**20,
    )
    gathering = [pltpu.VMEM((entries, width), F32), pltpu.VMEM((extent, width), BF16)]
    opening = call(
        functools.partial(opening_body, own, face), "opening_products",
        [IN_SMEM] + [IN_VMEM] * 3 + [IN_ANY],
        [
            shape((entries, width), F32), shape((entries, 2 * face), BF16),
            shape((face, 2 * face), BF16), shape((face, width), F32),
        ],
        gathering + [pltpu.VMEM(cell_matrices.shape, BF16), pltpu.SemaphoreType.DMA],
        8 * 10**9, 16 * 2**20, 45,
    )
    local = call(
        functools.partial(local_body, own, face), "local_products", [IN_SMEM] + [IN_VMEM] * 4,
        [shape((entries, width), F32), shape((face, width), F32)], gathering,
        5 * 10**9, 16 * 2**20,
    )
    returned = call(
        returned_body, "returned", [IN_VMEM] * 3, shape((face, width), F32), [], 10**8, 2**20,
    )
    assemble = call(
        assemble_body, "assembled", [IN_SMEM] + [IN_VMEM] * 4, wide,
        [
            pltpu.VMEM((copied * cell_nodes, width), F32),
            pltpu.VMEM((entries - copied * cell_nodes, 2 * width), BF16),
        ]
        + [pltpu.VMEM((extent, width), F32)] * copied,
        5 * 10**9, 16 * 2**20,
    )

    scaled = (mass_scale[:, None] * wavefunctions.astype(F32)).astype(BF16).astype(F32)
    scaled = jnp.pad(scaled, ((0, face), (0, 0)))
    rows = start(face_list, scaled)
    previous, current = None, wavefunctions
    for sweep in range(DEGREE):
        received = passed_along(rows, -1)
        if sweep == 0:
            products, spread, block, sent = opening(
                connectivity, links, column, scaled, cell_matrices
            )
        else:
            products, sent = local(connectivity, links, column, scaled, cell_matrices)
        arrived = passed_along(returned(sent, block, received), 1)
        summed = assemble(connectivity, links, products, spread, received)
        parts = (summed, arrived, mass)
        if sweep == DEGREE - 1:
            filtered, rounded = call(
                last_body, "filtered", [IN_VMEM] * 6, [wide, shape((own, width), BF16)], [],
                10**9, 6 * 2**20,
            )(faces, *parts, previous, current)
        elif sweep == 0:
            following, scaled, rows = call(
                first_body, "first_step", [IN_SMEM] + [IN_VMEM] * 5,
                [wide, scaled_shape, rows_shape], [picked], 10**9, 6 * 2**20,
            )(face_list, faces, *parts, current)
            previous, current = current, following
        else:
            following, scaled, rows = call(
                next_body, "next_step", [IN_SMEM] + [IN_VMEM] * 6,
                [wide, scaled_shape, rows_shape], [picked], 10**9, 6 * 2**20,
            )(face_list, faces, *parts, previous, current)
            previous, current = current, following

    chips, cores = lax.axis_size(CHIP), lax.axis_size(CORE)
    mine = exchanged(rounded.reshape(chips, own // chips, width), CHIP)
    both = exchanged(jnp.broadcast_to(mine, (cores, *mine.shape)), CORE)
    pairs = bands * (bands + 1) // 2
    half = pairs // cores
    core = lax.axis_index(CORE).astype(jnp.int32).reshape(1)
    gram = call(
        gram_body, "gram", [IN_SMEM, IN_VMEM], shape((half, width, width), BF16), [],
        10**9, 3 * 2**20,
    )(core, both)
    gram = sum_of_share(gram.reshape(half * width, width), PLANE)
    columns = lax.axis_size(COLUMN)
    gram = exchanged(jnp.broadcast_to(gram, (columns, *gram.shape)), COLUMN)
    gram = gram.astype(F32).sum(axis=0).astype(BF16)
    for axes in (PLANE, CORE):
        gram = shares_of_all(gram, axes)
    states = bands * width
    change, scale = call(
        functools.partial(correct_body, own * domains), "correction", [IN_SMEM, IN_VMEM, IN_VMEM],
        [shape(mine.shape, BF16), shape((8, width), F32)],
        [
            pltpu.VMEM((states, states), BF16),
            pltpu.VMEM((states, chips * width), BF16),
            pltpu.VMEM((states, chips * width), BF16),
        ],
        4 * 10**9, 8 * 2**20,
    )(core, gram.reshape(pairs, width, width), both)
    change = exchanged(change, CHIP).reshape(own, width)
    return call(finish_body, "rotated", [IN_VMEM] * 3, wide, [], 10**6, 3 * 2**20)(
        filtered, change, scale
    )


def solution(mesh):
    finer = Mesh(
        mesh.devices.reshape(4, 4, 2, 4, 2), ("dom_0", "dom_1", "dom_2", "band_0", "band_1")
    )
    placed = (P(DOM, BAND), P(DOM), P(DOM, None, None), P(DOM, None), P(DOM))
    return jax.shard_map(
        on_device, mesh=finer, in_specs=placed, out_specs=P(DOM, BAND), check_vma=False
    )
```

```python
import functools

import jax
import jax.numpy as jnp
from jax import lax
from jax.experimental import pallas as pl
from jax.experimental.pallas import tpu as pltpu
from jax.sharding import Mesh
from jax.sharding import PartitionSpec as P

STATES = 1024
DEGREE = 3
CENTER = 5.0
HALF = 5.0
DOM = ("dom_0", "dom_1", "dom_2")
BAND = ("band_0", "band_1")
PLANE = ("dom_0", "dom_1")
COLUMN = ("dom_2", "band_0")
CHIP = ("band_0",)
CORE = ("band_1",)
F32 = jnp.float32
BF16 = jnp.bfloat16
IN_VMEM = pl.BlockSpec(memory_space=pltpu.VMEM)
IN_SMEM = pl.BlockSpec(memory_space=pltpu.SMEM)
IN_ANY = pl.BlockSpec(memory_space=pl.ANY)


def shape(dims, dtype):
    return jax.ShapeDtypeStruct(dims, dtype)


def call(body, name, ins, outs, scratch=(), flops=0, moved=0, vmem=32):
    return pl.pallas_call(
        body,
        in_specs=ins,
        out_specs=jax.tree.map(lambda _: IN_VMEM, outs),
        out_shape=outs,
        scratch_shapes=list(scratch),
        compiler_params=pltpu.CompilerParams(vmem_limit_bytes=vmem * 2**20),
        cost_estimate=pl.CostEstimate(flops=flops, bytes_accessed=moved, transcendentals=0),
        name=name,
    )


def dot(a, b):
    return jnp.dot(a, b, preferred_element_type=F32)


def halves(a, axis=1):
    high = a.astype(BF16)
    return jnp.concatenate([high, (a - high.astype(F32)).astype(BF16)], axis)


def one_hot(hit):
    return jnp.where(hit, 1.0, 0.0).astype(BF16)


def pick_rows(face_ref, scaled_ref, rows_ref, picked):
    def take(i, carry):
        rows = [scaled_ref[pl.ds(face_ref[0, i * 8 + u], 1), :] for u in range(8)]
        picked[pl.ds(pl.multiple_of(i * 8, 8), 8), :] = jnp.concatenate(rows, 0)
        return carry

    lax.fori_loop(0, picked.shape[0] // 8, take, 0)
    rows_ref[...] = picked[...].astype(BF16)


def scale_rows(own, width, values, mass_ref, face_ref, scaled_ref, rows_ref, picked):
    scaled_ref[:own, :] = (mass_ref[...] * values).astype(BF16).astype(F32)
    scaled_ref[own:, :] = jnp.zeros((scaled_ref.shape[0] - own, width), F32)
    pick_rows(face_ref, scaled_ref, rows_ref, picked)


def face_hits(links_ref, own, face, cell, nodes):
    links = links_ref[:1, cell * nodes : (cell + 1) * nodes]
    return one_hot(links == lax.broadcasted_iota(jnp.int32, (face, nodes), 0) + own)


def take_entries(index_ref, column_ref, scaled_ref, held, narrow):
    cells, nodes = index_ref.shape
    extent, width = scaled_ref.shape
    copied = cells - column_ref.shape[0] // nodes
    narrow[...] = scaled_ref[...].astype(BF16)
    steps = 4
    some = nodes // steps
    rest = column_ref.shape[0] // steps

    def take(i, carry):
        first = pl.multiple_of(i * rest, rest)
        named = column_ref[pl.ds(first, rest), :]
        lane = lax.broadcasted_iota(jnp.int32, (rest, 128), 1)
        hits = jnp.concatenate([one_hot(named == lane + t) for t in range(0, extent, 128)], 1)
        product = dot(hits, narrow[...])
        for k in range(some // 8):
            for cell in range(copied):
                at = i * some + k * 8
                rows = [scaled_ref[pl.ds(index_ref[cell, at + u], 1), :] for u in range(8)]
                held[pl.ds(pl.multiple_of(cell * nodes + at, 8), 8), :] = jnp.concatenate(rows, 0)
        held[pl.ds(copied * nodes + first, rest), :] = product
        return carry

    lax.fori_loop(0, steps, take, 0)


def opening_body(
    own, face, index_ref, links_ref, column_ref, scaled_ref, matrices_ref, products_ref,
    spread_ref, block_ref, sent_ref, held, narrow, cells_ref, sem,
):
    copy = pltpu.make_async_copy(matrices_ref, cells_ref, sem)
    copy.start()
    take_entries(index_ref, column_ref, scaled_ref, held, narrow)
    copy.wait()
    cells, nodes = index_ref.shape
    width = scaled_ref.shape[1]
    total = jnp.zeros((face, 2 * width), F32)
    block = jnp.zeros((face, 2 * face), F32)
    for cell in range(cells):
        part = slice(cell * nodes, (cell + 1) * nodes)
        hits = face_hits(links_ref, own, face, cell, nodes)
        columns = lax.dot_general(
            cells_ref[cell], hits, (((1,), (1,)), ((), ())), preferred_element_type=F32
        )
        both = halves(columns)
        spread_ref[part, :] = both
        block = block + dot(hits, both)
        product = dot(cells_ref[cell], held[part, :].astype(BF16))
        products_ref[part, :] = product
        total = total + dot(hits, halves(product))
    sent_ref[...] = total[:, :width] + total[:, width:]
    block_ref[...] = halves(block[:, :face] + block[:, face:])


def local_body(
    own, face, index_ref, links_ref, column_ref, scaled_ref, cells_ref, products_ref, sent_ref,
    held, narrow,
):
    take_entries(index_ref, column_ref, scaled_ref, held, narrow)
    cells, nodes = index_ref.shape
    width = scaled_ref.shape[1]
    total = jnp.zeros((face, 2 * width), F32)
    for cell in range(cells):
        part = slice(cell * nodes, (cell + 1) * nodes)
        product = dot(cells_ref[cell], held[part, :].astype(BF16))
        products_ref[part, :] = product
        total = total + dot(face_hits(links_ref, own, face, cell, nodes), halves(product))
    sent_ref[...] = total[:, :width] + total[:, width:]


def returned_body(sent_ref, block_ref, rows_ref, total_ref):
    rows = rows_ref[...]
    total_ref[...] = sent_ref[...] + dot(block_ref[...], jnp.concatenate([rows, rows], 0))


def assemble_body(
    index_ref, links_ref, products_ref, spread_ref, rows_ref, summed_ref, whole, split, *totals
):
    cells, nodes = index_ref.shape
    own, width = summed_ref.shape
    added = len(totals)
    rows = rows_ref[...]
    twice = jnp.concatenate([rows, rows], 0)
    for cell in range(cells):
        part = slice(cell * nodes, (cell + 1) * nodes)
        product = products_ref[part, :] + dot(spread_ref[part, :], twice)
        if cell < added:
            whole[part, :] = product
        else:
            split[(cell - added) * nodes : (cell - added + 1) * nodes, :] = halves(product)
    for total in totals:
        total[...] = jnp.zeros_like(total)
    steps = 4
    some = nodes // steps
    tall = own // steps

    def add(i, carry):
        first = pl.multiple_of(i * tall, tall)
        row = lax.broadcasted_iota(jnp.int32, (tall, 128), 0) + first
        hits = jnp.concatenate(
            [
                one_hot(links_ref[:1, t : t + 128] == row)
                for t in range(added * nodes, cells * nodes, 128)
            ],
            1,
        )
        both = dot(hits, split[...])
        for u in range(some):
            j = i * some + u
            at = [pl.ds(index_ref[cell, j], 1) for cell in range(added)]
            sums = [
                totals[cell][at[cell], :] + whole[pl.ds(cell * nodes + j, 1), :]
                for cell in range(added)
            ]
            for cell in range(added):
                totals[cell][at[cell], :] = sums[cell]
        summed_ref[pl.ds(first, tall), :] = both[:, :width] + both[:, width:]
        return carry

    lax.fori_loop(0, steps, add, 0)

    def collect(i, carry):
        part = pl.ds(pl.multiple_of(i * 64, 64), 64)
        summed = summed_ref[part, :]
        for total in totals:
            summed = summed + total[part, :]
        summed_ref[part, :] = summed
        return carry

    lax.fori_loop(0, own // 64, collect, 0)


def applied(faces_ref, summed_ref, arrived_ref, mass_ref):
    own, width = summed_ref.shape
    face = arrived_ref.shape[0]
    hits = one_hot(lax.broadcasted_iota(jnp.int32, (own, face), 0) == faces_ref[:1, :])
    added = dot(hits, halves(arrived_ref[...]))
    return mass_ref[...] * (summed_ref[...] + (added[:, :width] + added[:, width:]))


def first_body(
    face_ref, faces_ref, summed_ref, arrived_ref, mass_ref, wave_ref,
    current_ref, scaled_ref, sent_ref, picked,
):
    own, width = summed_ref.shape
    image = applied(faces_ref, summed_ref, arrived_ref, mass_ref)
    current_ref[...] = (image - CENTER * wave_ref[...].astype(F32)) / HALF
    scale_rows(own, width, current_ref[...], mass_ref, face_ref, scaled_ref, sent_ref, picked)


def next_body(
    face_ref, faces_ref, summed_ref, arrived_ref, mass_ref, previous_ref,
    current_ref, following_ref, scaled_ref, sent_ref, picked,
):
    own, width = summed_ref.shape
    image = applied(faces_ref, summed_ref, arrived_ref, mass_ref)
    following_ref[...] = 2.0 * (image - CENTER * current_ref[...]) / HALF - previous_ref[
        ...
    ].astype(F32)
    scale_rows(own, width, following_ref[...], mass_ref, face_ref, scaled_ref, sent_ref, picked)


def last_body(
    faces_ref, summed_ref, arrived_ref, mass_ref, previous_ref, current_ref,
    filtered_ref, rounded_ref,
):
    image = applied(faces_ref, summed_ref, arrived_ref, mass_ref)
    filtered = 2.0 * (image - CENTER * current_ref[...]) / HALF - previous_ref[...].astype(F32)
    filtered_ref[...] = filtered
    rounded_ref[...] = filtered.astype(BF16)


def gram_body(core_ref, rows_ref, blocks_ref):
    cores, chips = rows_ref.shape[:2]
    width = rows_ref.shape[3]
    groups = chips * cores
    group = [rows_ref[g % cores, g // cores] for g in range(groups)]
    half = blocks_ref.shape[0]

    def blocks(first):
        at = 0
        for g in range(groups):
            wanted = [h for h in range(g, groups) if first <= at + h - g < first + half]
            if wanted:
                panel = lax.dot_general(
                    group[g], jnp.concatenate([group[h] for h in wanted], 1),
                    (((0,), (0,)), ((), ())), preferred_element_type=F32,
                )
                for i, h in enumerate(wanted):
                    blocks_ref[at + h - g - first] = panel[
                        :, i * width : (i + 1) * width
                    ].astype(BF16)
            at += groups - g

    for core in range(cores):
        pl.when(core_ref[0] == core)(functools.partial(blocks, core * half))


def correct_body(nodes, core_ref, blocks_ref, rows_ref, change_ref, scale_ref, excess, power, change):
    cores, chips, own, width = rows_ref.shape
    groups = chips * cores
    states = groups * width
    same = lax.broadcasted_iota(jnp.int32, (width, width), 0) == lax.broadcasted_iota(
        jnp.int32, (width, width), 1
    )
    places = [(g, h) for g in range(groups) for h in range(g, groups)]
    diagonal = jnp.zeros((width, width), F32)
    for at, (g, h) in enumerate(places):
        if g == h:
            diagonal = diagonal + jnp.where(same, blocks_ref[at].astype(F32), 0.0)
    trace = jnp.sum(jnp.sum(diagonal, axis=0, keepdims=True), axis=1, keepdims=True)
    unit = states / trace
    for at, (g, h) in enumerate(places):
        block = blocks_ref[at].astype(F32) * unit
        if g == h:
            block = block - same.astype(F32)
        block = block.astype(BF16)
        excess[g * width : (g + 1) * width, h * width : (h + 1) * width] = block
        if g != h:
            excess[h * width : (h + 1) * width, g * width : (g + 1) * width] = block.T
    scale = 1.0 / jnp.sqrt(trace / (states * nodes))
    scale_ref[...] = jnp.broadcast_to(scale, scale_ref.shape)

    count = change_ref.shape[1]
    some = pl.ds(pl.multiple_of(core_ref[0] * count, count), count)
    for g in range(groups):
        power[:, g * width : (g + 1) * width] = rows_ref[g % cores, g // cores, some, :]
    for factor in (-0.5, 0.375, -0.3125, 0.0625):
        product = dot(power[...], excess[...])
        power[...] = product.astype(BF16)
        if factor == -0.5:
            change[...] = factor * product
        else:
            change[...] += factor * product
    for g in range(groups):
        part = change[:, g * width : (g + 1) * width]
        change_ref[g] = (part * scale).astype(BF16)


def finish_body(filtered_ref, change_ref, scale_ref, rotated_ref):
    rotated_ref[...] = filtered_ref[...] * scale_ref[:1, :] + change_ref[...].astype(F32)


def passed_along(value, steps):
    count = lax.axis_size(DOM)
    initial, last = max(0, -steps), min(count, count - steps)
    return lax.ppermute(value, DOM, [(source, source + steps) for source in range(initial, last)])


def exchanged(pieces, axes):
    return lax.all_to_all(pieces, axes, split_axis=0, concat_axis=0, tiled=True)


def sum_of_share(array, axes):
    peers = lax.axis_size(axes)
    pieces = array.reshape(peers, array.shape[0] // peers, array.shape[1])
    return exchanged(pieces, axes).astype(F32).sum(axis=0).astype(BF16)


def shares_of_all(array, axes):
    peers = lax.axis_size(axes)
    arrived = exchanged(jnp.broadcast_to(array, (peers, *array.shape)), axes)
    return arrived.reshape(peers * array.shape[0], array.shape[1])


def on_device(wavefunctions, mass_scale, cell_matrices, connectivity, face_index):
    own, width = wavefunctions.shape
    face = face_index.shape[0]
    cells, cell_nodes = connectivity.shape
    extent = own + face
    entries = cells * cell_nodes
    domains = lax.axis_size(DOM)
    bands = lax.axis_size(BAND)

    mass = jnp.broadcast_to(mass_scale[:, None], (own, width))
    links = jnp.broadcast_to(connectivity.reshape(1, entries), (8, entries))
    copied = cells // 2
    column = jnp.broadcast_to(
        connectivity[copied:].reshape(-1, 1), ((cells - copied) * cell_nodes, 128)
    )
    faces = jnp.broadcast_to(face_index.reshape(1, face), (8, face))
    face_list = face_index.reshape(1, face)

    picked = pltpu.VMEM((face, width), F32)
    scaled_shape = shape((extent, width), F32)
    rows_shape = shape((face, width), BF16)
    wide = shape((own, width), F32)
    start = call(
        pick_rows, "face_rows", [IN_SMEM, IN_VMEM], rows_shape, [picked], 10**6, 2**20,
    )
    gathering = [pltpu.VMEM((entries, width), F32), pltpu.VMEM((extent, width), BF16)]
    opening = call(
        functools.partial(opening_body, own, face), "opening_products",
        [IN_SMEM] + [IN_VMEM] * 3 + [IN_ANY],
        [
            shape((entries, width), F32), shape((entries, 2 * face), BF16),
            shape((face, 2 * face), BF16), shape((face, width), F32),
        ],
        gathering + [pltpu.VMEM(cell_matrices.shape, BF16), pltpu.SemaphoreType.DMA],
        8 * 10**9, 16 * 2**20, 45,
    )
    local = call(
        functools.partial(local_body, own, face), "local_products", [IN_SMEM] + [IN_VMEM] * 4,
        [shape((entries, width), F32), shape((face, width), F32)], gathering,
        5 * 10**9, 16 * 2**20,
    )
    returned = call(
        returned_body, "returned", [IN_VMEM] * 3, shape((face, width), F32), [], 10**8, 2**20,
    )
    assemble = call(
        assemble_body, "assembled", [IN_SMEM] + [IN_VMEM] * 4, wide,
        [
            pltpu.VMEM((copied * cell_nodes, width), F32),
            pltpu.VMEM((entries - copied * cell_nodes, 2 * width), BF16),
        ]
        + [pltpu.VMEM((extent, width), F32)] * copied,
        5 * 10**9, 16 * 2**20,
    )

    scaled = (mass_scale[:, None] * wavefunctions.astype(F32)).astype(BF16).astype(F32)
    scaled = jnp.pad(scaled, ((0, face), (0, 0)))
    rows = start(face_list, scaled)
    previous, current = None, wavefunctions
    for sweep in range(DEGREE):
        received = passed_along(rows, -1)
        if sweep == 0:
            products, spread, block, sent = opening(
                connectivity, links, column, scaled, cell_matrices
            )
        else:
            products, sent = local(connectivity, links, column, scaled, cell_matrices)
        arrived = passed_along(returned(sent, block, received), 1)
        summed = assemble(connectivity, links, products, spread, received)
        parts = (summed, arrived, mass)
        if sweep == DEGREE - 1:
            filtered, rounded = call(
                last_body, "filtered", [IN_VMEM] * 6, [wide, shape((own, width), BF16)], [],
                10**9, 6 * 2**20,
            )(faces, *parts, previous, current)
        elif sweep == 0:
            following, scaled, rows = call(
                first_body, "first_step", [IN_SMEM] + [IN_VMEM] * 5,
                [wide, scaled_shape, rows_shape], [picked], 10**9, 6 * 2**20,
            )(face_list, faces, *parts, current)
            previous, current = current, following
        else:
            following, scaled, rows = call(
                next_body, "next_step", [IN_SMEM] + [IN_VMEM] * 6,
                [wide, scaled_shape, rows_shape], [picked], 10**9, 6 * 2**20,
            )(face_list, faces, *parts, previous, current)
            previous, current = current, following

    chips, cores = lax.axis_size(CHIP), lax.axis_size(CORE)
    mine = exchanged(rounded.reshape(chips, own // chips, width), CHIP)
    both = exchanged(jnp.broadcast_to(mine, (cores, *mine.shape)), CORE)
    pairs = bands * (bands + 1) // 2
    half = pairs // cores
    core = lax.axis_index(CORE).astype(jnp.int32).reshape(1)
    gram = call(
        gram_body, "gram", [IN_SMEM, IN_VMEM], shape((half, width, width), BF16), [],
        10**9, 3 * 2**20,
    )(core, both)
    gram = sum_of_share(gram.reshape(half * width, width), PLANE)
    columns = lax.axis_size(COLUMN)
    gram = exchanged(jnp.broadcast_to(gram, (columns, *gram.shape)), COLUMN)
    gram = gram.astype(F32).sum(axis=0).astype(BF16)
    for axes in (PLANE, CORE):
        gram = shares_of_all(gram, axes)
    states = bands * width
    change, scale = call(
        functools.partial(correct_body, own * domains), "correction", [IN_SMEM, IN_VMEM, IN_VMEM],
        [shape((bands, own // bands, width), BF16), shape((8, width), F32)],
        [
            pltpu.VMEM((states, states), BF16),
            pltpu.VMEM((own // bands, states), BF16),
            pltpu.VMEM((own // bands, states), F32),
        ],
        4 * 10**9, 8 * 2**20,
    )(core, gram.reshape(pairs, width, width), both)
    change = exchanged(change, BAND).reshape(own, width)
    return call(finish_body, "rotated", [IN_VMEM] * 3, wide, [], 10**6, 3 * 2**20)(
        filtered, change, scale
    )


def solution(mesh):
    finer = Mesh(
        mesh.devices.reshape(4, 4, 2, 4, 2), ("dom_0", "dom_1", "dom_2", "band_0", "band_1")
    )
    placed = (P(DOM, BAND), P(DOM), P(DOM, None, None), P(DOM, None), P(DOM))
    return jax.shard_map(
        on_device, mesh=finer, in_specs=placed, out_specs=P(DOM, BAND), check_vma=False
    )
```

```python
import functools

import jax
import jax.numpy as jnp
from jax import lax
from jax.experimental import pallas as pl
from jax.experimental.pallas import tpu as pltpu
from jax.sharding import Mesh
from jax.sharding import PartitionSpec as P

STATES = 1024
DEGREE = 3
CENTER = 5.0
HALF = 5.0
DOM = ("dom_0", "dom_1", "dom_2")
BAND = ("band_0", "band_1")
PLANE = ("dom_0", "dom_1")
COLUMN = ("dom_2", "band_0")
CHIP = ("band_0",)
CORE = ("band_1",)
F32 = jnp.float32
BF16 = jnp.bfloat16
IN_VMEM = pl.BlockSpec(memory_space=pltpu.VMEM)
IN_SMEM = pl.BlockSpec(memory_space=pltpu.SMEM)
IN_ANY = pl.BlockSpec(memory_space=pl.ANY)


def shape(dims, dtype):
    return jax.ShapeDtypeStruct(dims, dtype)


def call(body, name, ins, outs, scratch=(), flops=0, moved=0, vmem=32):
    return pl.pallas_call(
        body,
        in_specs=ins,
        out_specs=jax.tree.map(lambda _: IN_VMEM, outs),
        out_shape=outs,
        scratch_shapes=list(scratch),
        compiler_params=pltpu.CompilerParams(vmem_limit_bytes=vmem * 2**20),
        cost_estimate=pl.CostEstimate(flops=flops, bytes_accessed=moved, transcendentals=0),
        name=name,
    )


def dot(a, b):
    return jnp.dot(a, b, preferred_element_type=F32)


def halves(a, axis=1):
    high = a.astype(BF16)
    return jnp.concatenate([high, (a - high.astype(F32)).astype(BF16)], axis)


def one_hot(hit):
    return jnp.where(hit, 1.0, 0.0).astype(BF16)


def pick_rows(face_ref, scaled_ref, rows_ref, picked):
    def take(i, carry):
        rows = [scaled_ref[pl.ds(face_ref[0, i * 8 + u], 1), :] for u in range(8)]
        picked[pl.ds(pl.multiple_of(i * 8, 8), 8), :] = jnp.concatenate(rows, 0)
        return carry

    lax.fori_loop(0, picked.shape[0] // 8, take, 0)
    rows_ref[...] = picked[...].astype(BF16)


def scale_rows(own, width, values, mass_ref, face_ref, scaled_ref, rows_ref, picked):
    scaled_ref[:own, :] = (mass_ref[...] * values).astype(BF16).astype(F32)
    scaled_ref[own:, :] = jnp.zeros((scaled_ref.shape[0] - own, width), F32)
    pick_rows(face_ref, scaled_ref, rows_ref, picked)


def face_hits(links_ref, own, face, cell, nodes):
    links = links_ref[:1, cell * nodes : (cell + 1) * nodes]
    return one_hot(links == lax.broadcasted_iota(jnp.int32, (face, nodes), 0) + own)


def take_entries(index_ref, column_ref, scaled_ref, held, narrow):
    cells, nodes = index_ref.shape
    extent, width = scaled_ref.shape
    copied = cells - column_ref.shape[0] // nodes
    narrow[...] = scaled_ref[...].astype(BF16)
    steps = 2
    some = nodes // steps
    rest = column_ref.shape[0] // steps

    def take(i, carry):
        first = pl.multiple_of(i * rest, rest)
        named = column_ref[pl.ds(first, rest), :]
        lane = lax.broadcasted_iota(jnp.int32, (rest, 128), 1)
        hits = jnp.concatenate([one_hot(named == lane + t) for t in range(0, extent, 128)], 1)
        product = dot(hits, narrow[...])
        for k in range(some // 8):
            for cell in range(copied):
                at = i * some + k * 8
                rows = [scaled_ref[pl.ds(index_ref[cell, at + u], 1), :] for u in range(8)]
                held[pl.ds(pl.multiple_of(cell * nodes + at, 8), 8), :] = jnp.concatenate(rows, 0)
        held[pl.ds(copied * nodes + first, rest), :] = product
        return carry

    lax.fori_loop(0, steps, take, 0)


def opening_body(
    own, face, index_ref, links_ref, column_ref, scaled_ref, matrices_ref, products_ref,
    spread_ref, block_ref, sent_ref, held, narrow, cells_ref, sem,
):
    copy = pltpu.make_async_copy(matrices_ref, cells_ref, sem)
    copy.start()
    take_entries(index_ref, column_ref, scaled_ref, held, narrow)
    copy.wait()
    cells, nodes = index_ref.shape
    width = scaled_ref.shape[1]
    total = jnp.zeros((face, 2 * width), F32)
    block = jnp.zeros((face, 2 * face), F32)
    for cell in range(cells):
        part = slice(cell * nodes, (cell + 1) * nodes)
        hits = face_hits(links_ref, own, face, cell, nodes)
        columns = lax.dot_general(
            cells_ref[cell], hits, (((1,), (1,)), ((), ())), preferred_element_type=F32
        )
        both = halves(columns)
        spread_ref[part, :] = both
        block = block + dot(hits, both)
        product = dot(cells_ref[cell], held[part, :].astype(BF16))
        products_ref[part, :] = product
        total = total + dot(hits, halves(product))
    sent_ref[...] = total[:, :width] + total[:, width:]
    block_ref[...] = halves(block[:, :face] + block[:, face:])


def local_body(
    own, face, index_ref, links_ref, column_ref, scaled_ref, cells_ref, products_ref, sent_ref,
    held, narrow,
):
    take_entries(index_ref, column_ref, scaled_ref, held, narrow)
    cells, nodes = index_ref.shape
    width = scaled_ref.shape[1]
    total = jnp.zeros((face, 2 * width), F32)
    for cell in range(cells):
        part = slice(cell * nodes, (cell + 1) * nodes)
        product = dot(cells_ref[cell], held[part, :].astype(BF16))
        products_ref[part, :] = product
        total = total + dot(face_hits(links_ref, own, face, cell, nodes), halves(product))
    sent_ref[...] = total[:, :width] + total[:, width:]


def returned_body(sent_ref, block_ref, rows_ref, total_ref):
    rows = rows_ref[...]
    total_ref[...] = sent_ref[...] + dot(block_ref[...], jnp.concatenate([rows, rows], 0))


def assemble_body(
    index_ref, links_ref, products_ref, spread_ref, rows_ref, summed_ref, whole, split, *totals
):
    cells, nodes = index_ref.shape
    own, width = summed_ref.shape
    added = len(totals)
    rows = rows_ref[...]
    twice = jnp.concatenate([rows, rows], 0)
    for cell in range(cells):
        part = slice(cell * nodes, (cell + 1) * nodes)
        product = products_ref[part, :] + dot(spread_ref[part, :], twice)
        if cell < added:
            whole[part, :] = product
        else:
            split[(cell - added) * nodes : (cell - added + 1) * nodes, :] = halves(product)
    for total in totals:
        total[...] = jnp.zeros_like(total)
    steps = 4
    some = nodes // steps
    tall = own // steps

    def add(i, carry):
        first = pl.multiple_of(i * tall, tall)
        row = lax.broadcasted_iota(jnp.int32, (tall, 128), 0) + first
        hits = jnp.concatenate(
            [
                one_hot(links_ref[:1, t : t + 128] == row)
                for t in range(added * nodes, cells * nodes, 128)
            ],
            1,
        )
        both = dot(hits, split[...])
        for u in range(some):
            j = i * some + u
            at = [pl.ds(index_ref[cell, j], 1) for cell in range(added)]
            sums = [
                totals[cell][at[cell], :] + whole[pl.ds(cell * nodes + j, 1), :]
                for cell in range(added)
            ]
            for cell in range(added):
                totals[cell][at[cell], :] = sums[cell]
        summed_ref[pl.ds(first, tall), :] = both[:, :width] + both[:, width:]
        return carry

    lax.fori_loop(0, steps, add, 0)

    def collect(i, carry):
        part = pl.ds(pl.multiple_of(i * 64, 64), 64)
        summed = summed_ref[part, :]
        for total in totals:
            summed = summed + total[part, :]
        summed_ref[part, :] = summed
        return carry

    lax.fori_loop(0, own // 64, collect, 0)


def applied(faces_ref, summed_ref, arrived_ref, mass_ref):
    own, width = summed_ref.shape
    face = arrived_ref.shape[0]
    hits = one_hot(lax.broadcasted_iota(jnp.int32, (own, face), 0) == faces_ref[:1, :])
    added = dot(hits, halves(arrived_ref[...]))
    return mass_ref[...] * (summed_ref[...] + (added[:, :width] + added[:, width:]))


def first_body(
    face_ref, faces_ref, summed_ref, arrived_ref, mass_ref, wave_ref,
    current_ref, scaled_ref, sent_ref, picked,
):
    own, width = summed_ref.shape
    image = applied(faces_ref, summed_ref, arrived_ref, mass_ref)
    current_ref[...] = (image - CENTER * wave_ref[...].astype(F32)) / HALF
    scale_rows(own, width, current_ref[...], mass_ref, face_ref, scaled_ref, sent_ref, picked)


def next_body(
    face_ref, faces_ref, summed_ref, arrived_ref, mass_ref, previous_ref,
    current_ref, following_ref, scaled_ref, sent_ref, picked,
):
    own, width = summed_ref.shape
    image = applied(faces_ref, summed_ref, arrived_ref, mass_ref)
    following_ref[...] = 2.0 * (image - CENTER * current_ref[...]) / HALF - previous_ref[
        ...
    ].astype(F32)
    scale_rows(own, width, following_ref[...], mass_ref, face_ref, scaled_ref, sent_ref, picked)


def last_body(
    faces_ref, summed_ref, arrived_ref, mass_ref, previous_ref, current_ref,
    filtered_ref, rounded_ref,
):
    image = applied(faces_ref, summed_ref, arrived_ref, mass_ref)
    filtered = 2.0 * (image - CENTER * current_ref[...]) / HALF - previous_ref[...].astype(F32)
    filtered_ref[...] = filtered
    rounded_ref[...] = filtered.astype(BF16)


def gram_body(core_ref, rows_ref, blocks_ref):
    cores, chips = rows_ref.shape[:2]
    width = rows_ref.shape[3]
    groups = chips * cores
    group = [rows_ref[g % cores, g // cores] for g in range(groups)]
    half = blocks_ref.shape[0]

    def blocks(first):
        at = 0
        for g in range(groups):
            wanted = [h for h in range(g, groups) if first <= at + h - g < first + half]
            if wanted:
                panel = lax.dot_general(
                    group[g], jnp.concatenate([group[h] for h in wanted], 1),
                    (((0,), (0,)), ((), ())), preferred_element_type=F32,
                )
                for i, h in enumerate(wanted):
                    blocks_ref[at + h - g - first] = panel[
                        :, i * width : (i + 1) * width
                    ].astype(BF16)
            at += groups - g

    for core in range(cores):
        pl.when(core_ref[0] == core)(functools.partial(blocks, core * half))


def correct_body(nodes, core_ref, blocks_ref, rows_ref, change_ref, scale_ref, excess, power, change):
    cores, chips, own, width = rows_ref.shape
    groups = chips * cores
    states = groups * width
    same = lax.broadcasted_iota(jnp.int32, (width, width), 0) == lax.broadcasted_iota(
        jnp.int32, (width, width), 1
    )
    places = [(g, h) for g in range(groups) for h in range(g, groups)]
    diagonal = jnp.zeros((width, width), F32)
    for at, (g, h) in enumerate(places):
        if g == h:
            diagonal = diagonal + jnp.where(same, blocks_ref[at].astype(F32), 0.0)
    trace = jnp.sum(jnp.sum(diagonal, axis=0, keepdims=True), axis=1, keepdims=True)
    unit = states / trace
    for at, (g, h) in enumerate(places):
        block = blocks_ref[at].astype(F32) * unit
        if g == h:
            block = block - same.astype(F32)
        block = block.astype(BF16)
        excess[g * width : (g + 1) * width, h * width : (h + 1) * width] = block
        if g != h:
            excess[h * width : (h + 1) * width, g * width : (g + 1) * width] = block.T
    scale = 1.0 / jnp.sqrt(trace / (states * nodes))
    scale_ref[...] = jnp.broadcast_to(scale, scale_ref.shape)

    count = change_ref.shape[1]
    some = pl.ds(pl.multiple_of(core_ref[0] * count, count), count)
    for g in range(groups):
        power[:, g * width : (g + 1) * width] = rows_ref[g % cores, g // cores, some, :]
    for factor in (-0.5, 0.375, -0.3125, 0.0625):
        product = dot(power[...], excess[...])
        power[...] = product.astype(BF16)
        if factor == -0.5:
            change[...] = factor * product
        else:
            change[...] += factor * product
    for g in range(groups):
        part = change[:, g * width : (g + 1) * width]
        change_ref[g] = (part * scale).astype(BF16)


def finish_body(filtered_ref, change_ref, scale_ref, rotated_ref):
    rotated_ref[...] = filtered_ref[...] * scale_ref[:1, :] + change_ref[...].astype(F32)


def passed_along(value, steps):
    count = lax.axis_size(DOM)
    initial, last = max(0, -steps), min(count, count - steps)
    return lax.ppermute(value, DOM, [(source, source + steps) for source in range(initial, last)])


def exchanged(pieces, axes):
    return lax.all_to_all(pieces, axes, split_axis=0, concat_axis=0, tiled=True)


def sum_of_share(array, axes):
    peers = lax.axis_size(axes)
    pieces = array.reshape(peers, array.shape[0] // peers, array.shape[1])
    return exchanged(pieces, axes).astype(F32).sum(axis=0).astype(BF16)


def shares_of_all(array, axes):
    peers = lax.axis_size(axes)
    arrived = exchanged(jnp.broadcast_to(array, (peers, *array.shape)), axes)
    return arrived.reshape(peers * array.shape[0], array.shape[1])


def on_device(wavefunctions, mass_scale, cell_matrices, connectivity, face_index):
    own, width = wavefunctions.shape
    face = face_index.shape[0]
    cells, cell_nodes = connectivity.shape
    extent = own + face
    entries = cells * cell_nodes
    domains = lax.axis_size(DOM)
    bands = lax.axis_size(BAND)

    mass = jnp.broadcast_to(mass_scale[:, None], (own, width))
    links = jnp.broadcast_to(connectivity.reshape(1, entries), (8, entries))
    copied = cells // 2
    column = jnp.broadcast_to(
        connectivity[copied:].reshape(-1, 1), ((cells - copied) * cell_nodes, 128)
    )
    faces = jnp.broadcast_to(face_index.reshape(1, face), (8, face))
    face_list = face_index.reshape(1, face)

    picked = pltpu.VMEM((face, width), F32)
    scaled_shape = shape((extent, width), F32)
    rows_shape = shape((face, width), BF16)
    wide = shape((own, width), F32)
    start = call(
        pick_rows, "face_rows", [IN_SMEM, IN_VMEM], rows_shape, [picked], 10**6, 2**20,
    )
    gathering = [pltpu.VMEM((entries, width), F32), pltpu.VMEM((extent, width), BF16)]
    opening = call(
        functools.partial(opening_body, own, face), "opening_products",
        [IN_SMEM] + [IN_VMEM] * 3 + [IN_ANY],
        [
            shape((entries, width), F32), shape((entries, 2 * face), BF16),
            shape((face, 2 * face), BF16), shape((face, width), F32),
        ],
        gathering + [pltpu.VMEM(cell_matrices.shape, BF16), pltpu.SemaphoreType.DMA],
        8 * 10**9, 16 * 2**20, 45,
    )
    local = call(
        functools.partial(local_body, own, face), "local_products", [IN_SMEM] + [IN_VMEM] * 4,
        [shape((entries, width), F32), shape((face, width), F32)], gathering,
        5 * 10**9, 16 * 2**20,
    )
    returned = call(
        returned_body, "returned", [IN_VMEM] * 3, shape((face, width), F32), [], 10**8, 2**20,
    )
    assemble = call(
        assemble_body, "assembled", [IN_SMEM] + [IN_VMEM] * 4, wide,
        [
            pltpu.VMEM((copied * cell_nodes, width), F32),
            pltpu.VMEM((entries - copied * cell_nodes, 2 * width), BF16),
        ]
        + [pltpu.VMEM((extent, width), F32)] * copied,
        5 * 10**9, 16 * 2**20,
    )

    scaled = (mass_scale[:, None] * wavefunctions.astype(F32)).astype(BF16).astype(F32)
    scaled = jnp.pad(scaled, ((0, face), (0, 0)))
    rows = start(face_list, scaled)
    previous, current = None, wavefunctions
    for sweep in range(DEGREE):
        received = passed_along(rows, -1)
        if sweep == 0:
            products, spread, block, sent = opening(
                connectivity, links, column, scaled, cell_matrices
            )
        else:
            products, sent = local(connectivity, links, column, scaled, cell_matrices)
        arrived = passed_along(returned(sent, block, received), 1)
        summed = assemble(connectivity, links, products, spread, received)
        parts = (summed, arrived, mass)
        if sweep == DEGREE - 1:
            filtered, rounded = call(
                last_body, "filtered", [IN_VMEM] * 6, [wide, shape((own, width), BF16)], [],
                10**9, 6 * 2**20,
            )(faces, *parts, previous, current)
        elif sweep == 0:
            following, scaled, rows = call(
                first_body, "first_step", [IN_SMEM] + [IN_VMEM] * 5,
                [wide, scaled_shape, rows_shape], [picked], 10**9, 6 * 2**20,
            )(face_list, faces, *parts, current)
            previous, current = current, following
        else:
            following, scaled, rows = call(
                next_body, "next_step", [IN_SMEM] + [IN_VMEM] * 6,
                [wide, scaled_shape, rows_shape], [picked], 10**9, 6 * 2**20,
            )(face_list, faces, *parts, previous, current)
            previous, current = current, following

    chips, cores = lax.axis_size(CHIP), lax.axis_size(CORE)
    mine = exchanged(rounded.reshape(chips, own // chips, width), CHIP)
    both = exchanged(jnp.broadcast_to(mine, (cores, *mine.shape)), CORE)
    pairs = bands * (bands + 1) // 2
    half = pairs // cores
    core = lax.axis_index(CORE).astype(jnp.int32).reshape(1)
    gram = call(
        gram_body, "gram", [IN_SMEM, IN_VMEM], shape((half, width, width), BF16), [],
        10**9, 3 * 2**20,
    )(core, both)
    gram = sum_of_share(gram.reshape(half * width, width), PLANE)
    columns = lax.axis_size(COLUMN)
    gram = exchanged(jnp.broadcast_to(gram, (columns, *gram.shape)), COLUMN)
    gram = gram.astype(F32).sum(axis=0).astype(BF16)
    for axes in (PLANE, CORE):
        gram = shares_of_all(gram, axes)
    states = bands * width
    change, scale = call(
        functools.partial(correct_body, own * domains), "correction", [IN_SMEM, IN_VMEM, IN_VMEM],
        [shape((bands, own // bands, width), BF16), shape((8, width), F32)],
        [
            pltpu.VMEM((states, states), BF16),
            pltpu.VMEM((own // bands, states), BF16),
            pltpu.VMEM((own // bands, states), F32),
        ],
        4 * 10**9, 8 * 2**20,
    )(core, gram.reshape(pairs, width, width), both)
    change = exchanged(change, BAND).reshape(own, width)
    return call(finish_body, "rotated", [IN_VMEM] * 3, wide, [], 10**6, 3 * 2**20)(
        filtered, change, scale
    )


def solution(mesh):
    finer = Mesh(
        mesh.devices.reshape(4, 4, 2, 4, 2), ("dom_0", "dom_1", "dom_2", "band_0", "band_1")
    )
    placed = (P(DOM, BAND), P(DOM), P(DOM, None, None), P(DOM, None), P(DOM))
    return jax.shard_map(
        on_device, mesh=finer, in_specs=placed, out_specs=P(DOM, BAND), check_vma=False
    )
```
